32 devices in a mesh: dp: 4 (over y, core), expert: 8 (over z, x).
Axes of the slice: x: 2, y: 2, z: 4, core: 2. Of those that a mesh axis runs over, the one named last changes fastest.
Arguments:
- tokens: bfloat16 [12608, 512], P(('dp', 'expert')), may hold values from -6 to 6
- w_qkv: bfloat16 [512, 1536], P('dp', 'expert'), may hold values from -1 to 1
- w_out: bfloat16 [512, 512], P('dp', 'expert'), may hold values from -2 to 2
- w_router: bfloat16 [512, 8], P('dp', 'expert'), may hold values from -0.1875 to 0.1875
- norm_params: bfloat16 [4, 512], P(None, 'expert'), may hold values from -1 to 2
- w_in: bfloat16 [8, 512, 2048], P('expert', None, 'dp'), may hold values from -0.25 to 0.25
- w_down: bfloat16 [8, 2048, 512], P('expert', 'dp'), may hold values from -6 to 6
- routes: int32 [12608, 2], P(('dp', 'expert')), may hold values from 0 to 7, all different within a row; in each aligned block of 394 rows (0 to 393, 394 to 787, ...) at most 184 rows name the same one
- threshold: int32 [1], replicated, may hold values from 1 to 4
- cotangent: bfloat16 [12608, 512], P(('dp', 'expert')), may hold values from -6 to 6
Outputs:
- block_out: bfloat16 [12608, 512], P(('dp', 'expert'))
- grad_tokens: bfloat16 [12608, 512], P(('dp', 'expert'))
- grad_qkv: float32 [512, 1536], P('dp', 'expert')
- grad_out: float32 [512, 512], P('dp', 'expert')
- grad_router: float32 [512, 8], P('dp', 'expert')
- grad_norms: float32 [4, 512], P(None, 'expert')
- grad_in: float32 [8, 512, 2048], P('expert', None, 'dp')
- grad_down: float32 [8, 2048, 512], P('expert', 'dp')
- clipped_qkv: float32 [512, 1536], P('dp', 'expert')
- clip_factors: float32 [8], replicated
The draws below stay inside these ranges and needn't reach their ends.
Inputs may be any that keep to these rules, and one draw needn't show every extreme that they name: `routes`: each token names 2 different experts; in the rows of one device no expert is named by more than 184 rows, a bound that some block reaches there.
All inputs are finite; a program needn't handle non-finite values.
Results may differ from the reference program's by a relative error of at most 0.023.
Values may be sent and summed in bfloat16 or wider, within the bound.
A program may use at most 128 MiB of HBM per device.

```python
import math
import jax
import jax.numpy as jnp
import numpy as np
from jax import lax

D = 512
HEADS = 8
HEAD = 64
FF = 2048
SEQ = 197
TOP = 2
IMG_DEV = 2
EXPERTS = 8
TOK_DEV = 394
TOKENS = 12608
CAP = 184


def draw_w_qkv(key, part):
    key = jax.random.fold_in(key, 11)
    base_key, scale_key = jax.random.split(key)
    base_draw = jax.random.truncated_normal(base_key, -4.0, 4.0, (D, 3 * D), jnp.float32)
    head_scale = jnp.exp(jax.random.uniform(scale_key, (2, HEADS), jnp.float32, 0.0, 0.53))
    column_scale = jnp.concatenate([jnp.repeat(head_scale.reshape(-1), HEAD), jnp.ones((D,), jnp.float32)])
    return (base_draw * column_scale[None, :] * D ** (-0.5)).astype(jnp.bfloat16)


def draw_norm_params(key, part):
    key = jax.random.fold_in(key, 23)
    noise = jax.random.truncated_normal(key, -3.0, 3.0, (4, D), jnp.float32)
    level = jnp.array([1.0, 0.0, 1.0, 0.0], jnp.float32)[:, None]
    spread = jnp.array([0.15, 0.1, 0.15, 0.1], jnp.float32)[:, None]
    return (level + spread * noise).astype(jnp.bfloat16)


def shard_levels(rng, shape, pieces, least, high):
    gain = 1.0
    for position, blocks in pieces:
        heights = jax.random.uniform(jax.random.fold_in(jax.random.fold_in(rng, 6), position), (blocks,), jnp.float32, least / len(pieces), high / len(pieces))
        gain = gain * jnp.repeat(jnp.exp(heights), shape[position] // blocks).reshape((-1,) + (1,) * (len(shape) - 1 - position))
    return gain


def routed_block(stream_key, own, number, rows, number_of, top, reach, lean):
    sequence = jax.random.permutation(stream_key, number_of)
    packed, common = shares(number_of, rows * top, reach, lean, True), shares(number_of, rows * top, reach, lean, False)
    places = jnp.arange(number_of)

    def named(sizes, rotation):
        used = int((sizes > 0).sum())
        fixed = max(1, used // 4)
        moved = fixed + (places - fixed + rotation * (used - fixed)) % max(1, number_of - fixed)
        return jnp.zeros((number_of,), jnp.int32).at[sequence[jnp.where(places < fixed, places, moved)]].set(jnp.asarray(sizes, jnp.int32))

    sizes = jnp.where(number % 4 == 0, named(packed, number // 4), named(common, number - number // 4 - 1))
    mixed = jax.random.permutation(jax.random.fold_in(own, 3), number_of)
    donor, receiver = mixed[0:number_of // 2 * 2:2], mixed[1:number_of // 2 * 2:2]
    slack = jnp.minimum(sizes[donor] - 1, reach - sizes[receiver]) // 2
    slack = jnp.where((donor == sequence[0]) | (receiver == sequence[0]) | (sizes[receiver] == 0), 0, jnp.maximum(slack, 0))
    moved = jax.random.randint(jax.random.fold_in(own, 4), (number_of // 2,), 0, 1 << 20) % (slack + 1)
    sizes = sizes.at[donor].add(-moved).at[receiver].add(moved)
    members = jnp.searchsorted(jnp.cumsum(sizes), jnp.arange(rows * top), side="right").astype(jnp.int32)
    grid = members.reshape(top, rows).T
    grid = grid[jax.random.permutation(jax.random.fold_in(own, 1), rows)]
    rotation = jax.random.randint(jax.random.fold_in(own, 2), (rows, 1), 0, top)
    return jnp.take_along_axis(grid, (jnp.arange(top)[None, :] + rotation) % top, axis=1)


def shares(amount, total, limit, skew, full):
    loads = [(1 << 20) // math.isqrt(grade ** skew) + 1 for grade in range(1, amount + 1)]
    largest = limit if full else min(limit, max(-(-total // amount), total * loads[0] // sum(loads)))
    least = 1 if total - largest >= amount - 1 else 0
    counts, rest = [largest] + [least] * (amount - 1), total - largest - least * (amount - 1)
    while rest > 0:
        free = [i for i in range(1, amount) if counts[i] < largest] or [i for i in range(1, amount) if counts[i] < limit]
        whole, left = sum([loads[i] for i in free]), rest
        for i in free:
            more = min(limit - counts[i], max(1, left * loads[i] // whole), rest)
            counts[i] = counts[i] + more
            rest = rest - more
    return np.array(counts)


def normal_values(stream_key, extent, deviation, limit, cuts=(), held_as=jnp.bfloat16):
    drawn = jax.random.normal(stream_key, extent, jnp.float32) * deviation
    if len(cuts) > 0:
        drawn = shard_levels(stream_key, extent, cuts, -0.22, 0.18) * drawn
    return jnp.clip(drawn, min=-limit, max=limit).astype(held_as)


def setup_inputs(seed: int = 0) -> dict:
    key_list = jax.random.split(jax.random.key(seed), 11)
    tokens = normal_values(key_list[0], (TOKENS, D), 1.0, 6.0, ((0, 32),))
    w_qkv = draw_w_qkv(jax.random.fold_in(key_list[10], 71), 0)
    w_out = normal_values(key_list[2], (D, D), (D // 64) ** -0.5, 2.0, ((0, 4), (1, 8)))
    w_router = normal_values(key_list[3], (D, EXPERTS), (2 * D) ** -0.5, 0.1875, ((0, 4), (1, 8)))
    norm_params = draw_norm_params(jax.random.fold_in(key_list[10], 71), 0)
    w_in = normal_values(key_list[5], (EXPERTS, D, FF), D ** -0.5, 0.25, ((0, 8), (2, 4)))
    w_down = normal_values(key_list[6], (EXPERTS, FF, D), 1.0, 6.0, ((0, 8), (1, 4)))
    routes_keys = jax.random.split(jax.random.fold_in(key_list[7], 1), TOKENS // TOK_DEV)
    routes_turns = jax.random.permutation(jax.random.fold_in(key_list[7], 3), TOKENS // TOK_DEV)
    routes = jax.vmap(lambda own, number: routed_block(jax.random.fold_in(key_list[7], 2), own, number, TOK_DEV, EXPERTS, TOP, CAP, 2))(routes_keys, routes_turns).reshape((TOKENS, TOP))
    threshold = jax.random.randint(key_list[8], (1,), 1, 5).astype(jnp.int32)
    cotangent = normal_values(key_list[9], (TOKENS, D), 1.0, 6.0, ((0, 32),))
    return {"tokens": tokens, "w_qkv": w_qkv, "w_out": w_out, "w_router": w_router, "norm_params": norm_params, "w_in": w_in, "w_down": w_down, "routes": routes, "threshold": threshold, "cotangent": cotangent}


EPS = 1e-06
LEARN = 0.001

@jax.custom_vjp
def low(v):
    return lax.optimization_barrier(v.astype(jnp.bfloat16)).astype(jnp.float32)

@jax.custom_vjp
def low_back(v):
    return v

def low_keep(v):
    return (low(v), None)

def low_pass(kept, grad):
    return (grad,)

def back_keep(v):
    return (v, None)

def back_low(kept, grad):
    return (low(grad),)
low.defvjp(low_keep, low_pass)
low_back.defvjp(back_keep, back_low)

def layer_norm(values, norm_gain, norm_shift):
    center = lax.optimization_barrier(jnp.mean(values, axis=-1, keepdims=True))
    centered = values - center
    spread = lax.optimization_barrier(jnp.mean(centered * centered, axis=-1, keepdims=True))
    return centered * lax.rsqrt(spread + EPS) * norm_gain + norm_shift

def attend(qkv_rows):
    images = qkv_rows.shape[0] // SEQ
    rounded = low_back(low(qkv_rows)).reshape(images, SEQ, 3, HEADS, HEAD)
    queries, key_part, values = (rounded[:, :, 0], rounded[:, :, 1], rounded[:, :, 2])
    scores = low_back(jnp.einsum('bqhd,bkhd->bhqk', queries, key_part, precision=lax.Precision.HIGHEST) * HEAD ** (-0.5))
    head_peaks = lax.optimization_barrier(jnp.max(scores, axis=(0, 2, 3)))
    probs = jax.nn.softmax(scores, axis=-1)
    attn_mixed = jnp.einsum('bhqk,bkhd->bqhd', low(probs), values, precision=lax.Precision.HIGHEST)
    return (low_back(low(attn_mixed.reshape(images * SEQ, D))), head_peaks)

def slot_targets(block_routes):
    flat_routes = block_routes.reshape(-1)
    onehot = (flat_routes[:, None] == jnp.arange(EXPERTS, dtype=jnp.int32)[None, :]).astype(jnp.int32)
    before = jnp.cumsum(onehot, axis=0) - onehot
    return flat_routes * CAP + lax.optimization_barrier(jnp.sum(before * onehot, axis=1))

def place_rows(rows_in, slot_index):
    return jnp.zeros((EXPERTS * CAP, D), rows_in.dtype).at[slot_index].set(rows_in)

def pick_rows(rows_in, slot_index):
    return rows_in[slot_index]

def reference(tokens, w_qkv, w_out, w_router, norm_params, w_in, w_down, routes, threshold, cotangent):
    blocks = TOKENS // TOK_DEV
    targets = jax.vmap(slot_targets)(routes.reshape(blocks, TOK_DEV, TOP)).astype(jnp.int32)

    def forward(source, qkv_weight, out_weight, router_weight, norm_gains, in_weight, down_weight):
        first_norm = layer_norm(source, norm_gains[0], norm_gains[1])
        qkv_rows = jnp.dot(low(first_norm), qkv_weight, precision=lax.Precision.HIGHEST)
        grouped = qkv_rows.reshape(-1, IMG_DEV * 8 * SEQ, 3 * D)
        attn_mixed, head_peaks = lax.map(jax.checkpoint(attend), grouped)
        attn_mixed = attn_mixed.reshape(TOKENS, D)
        resid = source + low_back(jnp.dot(attn_mixed, out_weight, precision=lax.Precision.HIGHEST))
        second_norm = low(layer_norm(resid, norm_gains[2], norm_gains[3]))
        probs = jax.nn.softmax(jnp.dot(second_norm, router_weight, precision=lax.Precision.HIGHEST), axis=-1)
        gate_weights = jnp.take_along_axis(probs, routes, axis=1)
        spread_rows = low_back(jnp.repeat(second_norm.reshape(blocks, TOK_DEV, D), TOP, axis=1))
        buffers = jax.vmap(place_rows)(spread_rows, targets).reshape(blocks, EXPERTS, CAP, D)

        def expert_block(rows_in):
            hidden = low_back(jnp.einsum('ecd,edf->ecf', rows_in, in_weight, precision=lax.Precision.HIGHEST))
            active = low(jax.nn.gelu(hidden, approximate=False))
            return low_back(low(jnp.einsum('ecf,efd->ecd', active, down_weight, precision=lax.Precision.HIGHEST)))
        results = lax.map(jax.checkpoint(expert_block), buffers)
        picked = jax.vmap(pick_rows)(results.reshape(blocks, EXPERTS * CAP, D), targets)
        moe_part = lax.optimization_barrier(jnp.sum(picked.reshape(TOKENS, TOP, D) * gate_weights[:, :, None], axis=1))
        return (resid + moe_part, lax.optimization_barrier(jnp.max(head_peaks, axis=0)))
    primals = (tokens.astype(jnp.float32), w_qkv.astype(jnp.float32), w_out.astype(jnp.float32), w_router.astype(jnp.float32), norm_params.astype(jnp.float32), w_in.astype(jnp.float32), w_down.astype(jnp.float32))
    output, pull, peak_logit = jax.vjp(forward, *primals, has_aux=True)
    grads = pull(cotangent.astype(jnp.float32))
    factors = jnp.sqrt(jnp.minimum(1.0, threshold[0].astype(jnp.float32) / peak_logit))
    head_scale = jnp.repeat(factors, HEAD)
    column_scale = jnp.concatenate([head_scale, head_scale, jnp.ones((D,), jnp.float32)])
    clipped = (primals[1] - LEARN * grads[1]) * column_scale[None, :]
    return (output.astype(jnp.bfloat16), grads[0].astype(jnp.bfloat16), grads[1], grads[2], grads[3], grads[4], grads[5], grads[6], clipped, factors)
```

```python
import functools

import jax
import jax.numpy as jnp
from jax import lax
from jax.experimental import pallas as pl
from jax.experimental.pallas import tpu as pltpu
from jax.sharding import PartitionSpec as P

D = 512
HEADS = 8
HEAD = 64
SEQ = 197
EPS = 1e-06
LEARN = 0.001
SEQP = 208
BF = jnp.bfloat16
F32 = jnp.float32
MESH = pl.DeviceIdType.MESH

(DENSE_E, DENSE_Y, DENSE_C, EXPW, COT, ACT, GATE, DXE, ZED, DGATE, WGC, WGY, RSC, RSY, RSE, SMC, SME) = range(17)


def dg(left, right, left_dim, right_dim):
    return lax.dot_general(
        left, right, (((left_dim,), (right_dim,)), ((), ())), preferred_element_type=F32
    )


def iota(shape, dim):
    return lax.broadcasted_iota(jnp.int32, shape, dim)


def eye(size, dtype=BF):
    return (iota((size, size), 0) == iota((size, size), 1)).astype(F32).astype(dtype)


def split_two(value):
    high = value.astype(BF)
    return high, (value - high.astype(F32)).astype(BF)


def to_row(column):
    size = column.shape[0]
    return jnp.sum(jnp.where(iota((size, size), 0) == iota((size, size), 1), column, 0.0), axis=0, keepdims=True)


def to_column(row):
    size = row.shape[1]
    return jnp.sum(jnp.where(iota((size, size), 0) == iota((size, size), 1), row, 0.0), axis=1, keepdims=True)


def norm_parts(values):
    centered = values - jnp.mean(values, axis=-1, keepdims=True)
    inverse = lax.rsqrt(jnp.mean(centered * centered, axis=-1, keepdims=True) + EPS)
    return centered * inverse, inverse


def norm_back(upstream, normed, inverse, gain):
    scaled = upstream * gain
    inner = scaled - jnp.mean(scaled, axis=-1, keepdims=True)
    inner = inner - normed * jnp.mean(scaled * normed, axis=-1, keepdims=True)
    return (
        inverse * inner,
        jnp.sum(upstream * normed, axis=0, keepdims=True),
        jnp.sum(upstream, axis=0, keepdims=True),
    )


def normal_parts(u):
    size = jnp.abs(u)
    t = 1.0 / (1.0 + (0.3275911 * 2.0 ** -0.5) * size)
    poly = t * (0.254829592 + t * (-0.284496736 + t * (1.421413741 + t * (-1.453152027 + t * 1.061405429))))
    bell = jnp.exp(-0.5 * u * u)
    tail = 0.5 * poly * bell
    return jnp.where(u >= 0, 1.0 - tail, tail), u * (bell * 0.3989422804014327)


def block_kernel(
    n_e, cap, rows,
    tok, cot, routes, w_qkv, w_out, w_router, norm, win, wdown, threshold,
    block_out, grad_tok, grad_qkv, grad_out, grad_router, grad_norm, grad_in, grad_down, clipped, factors,
    GB, WI, WD, XF, CP, R, A1, A2, QKV, O, PS, SEL, SELT, SLOT, NRM, PR, WR,
    SA, SB, CR, AR, ZR, DXR, GS, GR, GCOL, DGS, DGR, H, DU, DZ,
    WCS, WCR, WYS, WYR, DQKV, DO, DR, GG, RCR, RYS, RYR, RES, RER, SM, SMCR, SMER,
    send, recv, local,
):
    dp = lax.axis_index("dp")
    me = lax.axis_index("expert")
    core = lax.rem(dp, 2)
    dp_c = dp + 1 - 2 * core
    dp_y = lax.rem(dp + 2, 4)
    dp_cy = lax.rem(dp_c + 2, 4)
    images = rows // SEQ
    T = images * SEQP
    part = 3 * D // n_e
    opart = D // n_e
    bundle = part + opart + 16

    def at_off(i):
        return lax.rem(me + i, n_e)

    def from_off(i):
        return lax.rem(me + n_e - i, n_e)

    def remote(src, dst, kind, i, where):
        return pltpu.make_async_remote_copy(
            src_ref=src, dst_ref=dst, send_sem=send.at[kind, i], recv_sem=recv.at[kind, i],
            device_id=where, device_id_type=MESH,
        )

    def brow(e, start=0, size=None):
        return pl.ds(pl.multiple_of(bundle * e + start, 16), bundle if size is None else size)

    peers = [(dp, at_off(i)) for i in range(1, n_e)] + [(dp_y, me), (dp_c, me)]
    barrier = pltpu.get_barrier_semaphore()
    for p in peers:
        pl.semaphore_signal(barrier, inc=1, device_id=p, device_id_type=MESH)
    load_in = pltpu.make_async_copy(win, WI.at[dp], local.at[0])
    load_down = pltpu.make_async_copy(wdown, WD.at[dp], local.at[1])
    load_in.start()
    load_down.start()

    GB[dp, brow(me, 0, part), :] = dg(eye(part), w_qkv[...], 1, 1).astype(BF)
    GB[dp, brow(me, part, opart), :] = dg(eye(opart), w_out[...], 1, 1).astype(BF)
    spread = (iota((16, 4), 0) == iota((16, 4), 1)).astype(F32).astype(BF)
    twice = (lax.rem(iota((HEAD, 128), 1), HEAD) == iota((HEAD, 128), 0)).astype(F32).astype(BF)
    small = dg(dg(spread, norm[...], 1, 0).astype(BF), twice, 1, 0)
    router_row = to_row(w_router[...].astype(F32))
    small = jnp.where(iota((16, 128), 0) == 8, router_row, small)
    GB[dp, brow(me, part + opart, 16), :] = small.astype(BF)

    pl.semaphore_wait(barrier, len(peers))

    def dense_e(i, e, where):
        return remote(GB.at[dp, brow(e)], GB.at[dp, brow(e)], DENSE_E, i, where)

    def dense_y(i):
        e = from_off(i)
        return remote(GB.at[dp, brow(e)], GB.at[dp, brow(e)], DENSE_Y, i, (dp_y, me))

    def dense_c(i):
        d = dp if i == 0 else dp_y
        return remote(GB.at[d], GB.at[d], DENSE_C, i, (dp_c, me))

    for i in range(1, n_e):
        dense_e(i, me, (dp, at_off(i))).start()
    dense_y(0).start()

    move = ((lax.div(iota((T, rows), 0), SEQP) * SEQ + lax.rem(iota((T, rows), 0), SEQP) == iota((T, rows), 1))
            & (lax.rem(iota((T, rows), 0), SEQP) < SEQ)).astype(F32).astype(BF)
    CP[...] = dg(move, cot[...], 1, 0).astype(BF)
    XF[...] = dg(move, tok[...], 1, 0)
    away = routes[...] - me
    away = jnp.where(away < 0, away + n_e, away)
    named = (away[:, 0:1] == iota((rows, n_e), 1)) | (away[:, 1:2] == iota((rows, n_e), 1))
    chosen = dg(move, named.astype(F32).astype(BF), 1, 0)
    before = (iota((T, T), 1) < iota((T, T), 0)).astype(F32).astype(BF)
    chosen_low = chosen.astype(BF)
    slot = jnp.where(chosen > 0.5, dg(before, chosen_low, 1, 0), -1.0)
    SLOT[...] = slot
    chosen_t = dg(eye(n_e), chosen_low, 1, 1)
    slot_t = jnp.where(chosen_t > 0.5, dg(chosen_t.astype(BF), before, 1, 1), -1.0)
    lane = iota((T, 2 * cap), 1).astype(F32)
    for k in range(n_e // 2):
        target = jnp.where(lane < cap, slot[:, 2 * k:2 * k + 1], slot[:, 2 * k + 1:2 * k + 2] + cap)
        SELT[:, 2 * cap * k:2 * cap * (k + 1)] = (lane == target).astype(F32).astype(BF)
    level = iota((cap, T), 0).astype(F32)
    for i in range(n_e):
        SEL[i] = (level == slot_t[i:i + 1, :]).astype(F32).astype(BF)
        packed = dg(SEL[i], CP[...], 1, 0).astype(BF)
        if i == 0:
            CR[0:cap] = packed
        else:
            SA[cap * i:cap * (i + 1)] = packed

    for i in range(1, n_e):
        dense_e(i, from_off(i), (dp, at_off(i))).wait_recv()
        dense_y(i).start()
    dense_c(0).start()

    load_in.wait()
    load_down.wait()

    def exp_w(k):
        buf = WI if k % 2 == 0 else WD
        if k < 2:
            return remote(buf.at[dp], buf.at[dp], EXPW, k, (dp_y, me))
        d = dp if k < 4 else dp_y
        return remote(buf.at[d], buf.at[d], EXPW, k, (dp_c, me))

    for k in range(4):
        exp_w(k).start()

    def to_expert(buf_s, buf_r, kind, i):
        return remote(buf_s.at[pl.ds(cap * i, cap)], buf_r.at[pl.ds(cap * i, cap)], kind, i, (dp, at_off(i)))

    def to_token(buf_s, buf_r, kind, i):
        return remote(buf_s.at[pl.ds(cap * i, cap)], buf_r.at[pl.ds(cap * i, cap)], kind, i, (dp, from_off(i)))

    for i in range(1, n_e):
        to_expert(SA, CR, COT, i).start()

    half = iota((16, 128), 1) < HEAD
    pieces = []
    for k in range(D // 128):
        even = GB[dp, brow(2 * k, part + opart, 16), :].astype(F32)
        odd = GB[dp, brow(2 * k + 1, part + opart, 16), :].astype(F32)
        pieces.append(jnp.where(half, even, odd))
    NRM[...] = jnp.concatenate(pieces, axis=1)
    normed, _ = norm_parts(XF[...])
    A1[...] = (normed * NRM[0:1] + NRM[1:2]).astype(BF)

    for i in range(n_e):
        dense_y(i).wait_recv()
    dense_c(1).start()
    dense_c(0).wait_recv()
    dense_c(1).wait_recv()

    def dense_rows(e, start, size):
        return jnp.concatenate([GB[d, brow(e, start, size), :] for d in range(4)], axis=1)

    def qkv_weight(k):
        return jnp.concatenate([dense_rows(2 * k, 0, part), dense_rows(2 * k + 1, 0, part)], axis=0)

    def out_weight():
        return jnp.concatenate([dense_rows(e, part, opart) for e in range(n_e)], axis=0)

    for k in range(n_e // 2):
        QKV[:, 2 * part * k:2 * part * (k + 1)] = dg(A1[...], qkv_weight(k), 1, 1).astype(BF)

    row_ok = iota((SEQP, SEQP), 0) < SEQ
    col_ok = iota((SEQP, SEQP), 1) < SEQ
    first_head = iota((1, 128), 1) < HEAD
    masks = [first_head.astype(F32).astype(BF), (~first_head).astype(F32).astype(BF)]

    def attend(g, peaks):
        img = lax.div(g, HEADS // 2)
        pair = lax.rem(g, HEADS // 2)
        at = pl.ds(pl.multiple_of(SEQP * img, 16), SEQP)
        q2 = QKV[at, pl.ds(pl.multiple_of(128 * pair, 128), 128)]
        k2 = QKV[at, pl.ds(pl.multiple_of(D + 128 * pair, 128), 128)]
        v2 = QKV[at, pl.ds(pl.multiple_of(2 * D + 128 * pair, 128), 128)]
        mixed = jnp.zeros((SEQP, 128), F32)
        for hh in range(2):
            s = dg(q2 * masks[hh], k2, 1, 1) * HEAD ** -0.5
            s = jnp.where(col_ok, s, -1e30)
            top = jnp.max(s, axis=1, keepdims=True)
            ex = jnp.exp(s - top)
            p = ex / jnp.sum(ex, axis=1, keepdims=True)
            PS[2 * g + hh] = p
            mixed = mixed + dg(p.astype(BF), v2 * masks[hh], 1, 0)
            peak = jnp.max(jnp.where(row_ok, s, -1e30), axis=(0, 1), keepdims=True)
            peaks = jnp.where(iota((8, 128), 0) == 2 * pair + hh, jnp.maximum(peaks, peak), peaks)
        O[at, pl.ds(pl.multiple_of(128 * pair, 128), 128)] = mixed.astype(BF)
        return peaks

    peaks = lax.fori_loop(0, images * HEADS // 2, attend, jnp.full((8, 128), -1e30, F32))
    for k in range(D // 128):
        SM[0, k, 8:16, :] = peaks

    for k in range(2):
        exp_w(k).wait_recv()
        exp_w(4 + k).start()

    R[...] = XF[...] + dg(O[...], out_weight(), 1, 1)
    normed, _ = norm_parts(R[...])
    A2[...] = (normed * NRM[2:3] + NRM[3:4]).astype(BF)
    router = jnp.zeros((n_e, D), F32)
    for i in range(n_e):
        at = dense_rows(at_off(i), part + opart, 16).astype(F32)
        router = jnp.where(iota((n_e, D), 0) == i, at[8:9, :], router)
    WR[...] = router.astype(BF)
    logits = dg(A2[...], WR[...], 1, 1)
    ex = jnp.exp(logits - jnp.max(logits, axis=1, keepdims=True))
    PR[...] = ex / jnp.sum(ex, axis=1, keepdims=True)
    lane_cap = iota((T, cap), 1).astype(F32)
    for i in range(n_e):
        packed = dg(SEL[i], A2[...], 1, 0).astype(BF)
        gate = jnp.sum(jnp.where(lane_cap == SLOT[:, i:i + 1], PR[:, i:i + 1], 0.0), axis=0, keepdims=True)
        if i == 0:
            AR[0:cap] = packed
            GR[0] = jnp.broadcast_to(gate, (8, cap))
        else:
            SB[cap * i:cap * (i + 1)] = packed
            GS[i] = jnp.broadcast_to(gate, (8, cap))
            remote(GS.at[i], GR.at[i], GATE, i, (dp, at_off(i))).start()
            to_expert(SB, AR, ACT, i).start()

    for k in range(2, 6):
        exp_w(k).wait_recv()

    pairs = n_e // 2
    for j in range(pairs):
        mine = pl.ds(2 * cap * j, 2 * cap)
        gates = []
        for i in (2 * j, 2 * j + 1):
            if i > 0:
                to_expert(SA, CR, COT, i).wait_recv()
                remote(GS.at[i], GR.at[i], GATE, i, (dp, at_off(i))).wait_recv()
                to_expert(SB, AR, ACT, i).wait_recv()
                to_expert(SA, CR, COT, i).wait_send()
                to_expert(SB, AR, ACT, i).wait_send()
            gates.append(to_column(GR[i, 0:1, :]))
        gate = jnp.concatenate(gates, axis=0)
        GCOL[...] = gate
        DZ[mine] = (CR[mine].astype(F32) * gate).astype(BF)

        def hidden(q, carry):
            d = lax.div(q, 2)
            at = pl.ds(pl.multiple_of(256 * lax.rem(q, 2), 256), 256)
            to = pl.ds(pl.multiple_of(256 * q, 256), 256)
            u = dg(AR[mine], WI[d, :, at], 1, 0)
            dh = dg(CR[mine], WD[d, at, :], 1, 1)
            phi, slope = normal_parts(u)
            H[mine, to] = (u * phi).astype(BF)
            DU[mine, to] = (dh * (phi + slope) * GCOL[...]).astype(BF)
            return carry

        lax.fori_loop(0, 8, hidden, 0)
        z = jnp.zeros((2 * cap, D), F32)
        dx = jnp.zeros((2 * cap, D), F32)
        for d in range(4):
            z = z + dg(H[mine, 512 * d:512 * (d + 1)], WD[d], 1, 0)
            dx = dx + dg(DU[mine, 512 * d:512 * (d + 1)], WI[d], 1, 1)
        z_low = z.astype(BF).astype(F32)
        dgate = jnp.sum(CR[mine].astype(F32) * z_low, axis=1, keepdims=True)
        z_out = (z_low * gate).astype(BF)
        dx_out = dx.astype(BF)
        for b, i in enumerate((2 * j, 2 * j + 1)):
            row = jnp.broadcast_to(to_row(dgate[cap * b:cap * (b + 1)]), (8, cap))
            if i == 0:
                DXR[0:cap] = dx_out[:cap]
                ZR[0:cap] = z_out[:cap]
                DGR[0] = row
            else:
                at = pl.ds(cap * i, cap)
                SB[at] = dx_out[cap * b:cap * (b + 1)]
                SA[at] = z_out[cap * b:cap * (b + 1)]
                DGS[i] = row
                remote(DGS.at[i], DGR.at[i], DGATE, i, (dp, from_off(i))).start()
                to_token(SB, DXR, DXE, i).start()
    for i in range(1, n_e):
        to_token(SA, ZR, ZED, i).start()

    def wg(d, w):
        at = pl.ds(pl.multiple_of(512 * d, 512), 512)
        if w == 0:
            return dg(AR[...], DU[:, at], 0, 0)
        return dg(H[:, at], DZ[...], 0, 0)

    yy = lax.div(dp, 2)

    def wgc(jy, w):
        return remote(WCS.at[2 * jy + w], WCR.at[2 * jy + w], WGC, 2 * jy + w, (dp_c, me))

    def wgy(w):
        return remote(WYS.at[w], WYR.at[w], WGY, w, (dp_y, me))

    for jy in (1, 0):
        for w in range(2):
            WCS[2 * jy + w] = wg(lax.rem(yy + jy, 2) * 2 + 1 - core, w).astype(BF)
            wgc(jy, w).start()
    for w in range(2):
        total = wg(dp_y, w)
        wgc(1, w).wait_recv()
        WYS[w] = (total + WCR[2 + w].astype(F32)).astype(BF)
        wgy(w).start()
    for w, out in enumerate((grad_in, grad_down)):
        total = wg(dp, w)
        wgc(0, w).wait_recv()
        out[...] = total + WCR[w].astype(F32)

    for i in range(1, n_e):
        remote(DGS.at[i], DGR.at[i], DGATE, i, (dp, from_off(i))).wait_recv()
        to_token(SB, DXR, DXE, i).wait_recv()
    lane_e = iota((T, n_e), 1)
    dprob = jnp.zeros((T, n_e), F32)
    for i in range(n_e):
        got = jnp.sum(jnp.where(lane_cap == SLOT[:, i:i + 1], DGR[i, 0:1, :], 0.0), axis=1, keepdims=True)
        dprob = jnp.where(lane_e == i, got, dprob)
    prob = PR[...]
    dlogit = prob * (dprob - jnp.sum(dprob * prob, axis=1, keepdims=True))
    high, low = split_two(dlogit)
    da2 = dg(SELT[...], DXR[...], 1, 0) + dg(high, WR[...], 1, 0) + dg(low, WR[...], 1, 0)
    g_router = dg(high, A2[...], 0, 0) + dg(low, A2[...], 0, 0)
    normed, inverse = norm_parts(R[...])
    back, g_gain2, g_shift2 = norm_back(da2, normed, inverse, NRM[2:3])
    DR[...] = CP[...].astype(F32) + back
    dy = DR[...].astype(BF)
    DO[...] = dg(dy, out_weight(), 1, 0).astype(BF)
    g_out = dg(dy, O[...], 0, 0).astype(BF)

    def attend_back(g, carry):
        img = lax.div(g, HEADS // 2)
        pair = lax.rem(g, HEADS // 2)
        at = pl.ds(pl.multiple_of(SEQP * img, 16), SEQP)
        cq = pl.ds(pl.multiple_of(128 * pair, 128), 128)
        ck = pl.ds(pl.multiple_of(D + 128 * pair, 128), 128)
        cv = pl.ds(pl.multiple_of(2 * D + 128 * pair, 128), 128)
        q2, k2, v2, do2 = QKV[at, cq], QKV[at, ck], QKV[at, cv], DO[at, cq]
        dq = dk = dv = jnp.zeros((SEQP, 128), F32)
        for hh in range(2):
            p = PS[2 * g + hh]
            do_h = do2 * masks[hh]
            dpr = dg(do_h, v2, 1, 1)
            ds = (p * (dpr - jnp.sum(dpr * p, axis=1, keepdims=True))).astype(BF)
            dq = dq + dg(ds, k2 * masks[hh], 1, 0)
            dk = dk + dg(ds, q2 * masks[hh], 0, 0)
            dv = dv + dg(p.astype(BF), do_h, 0, 0)
        DQKV[at, cq] = (dq * HEAD ** -0.5).astype(BF)
        DQKV[at, ck] = (dk * HEAD ** -0.5).astype(BF)
        DQKV[at, cv] = dv.astype(BF)
        return carry

    lax.fori_loop(0, images * HEADS // 2, attend_back, 0)

    for k in range(n_e // 2):
        g2 = dg(DQKV[:, 2 * part * k:2 * part * (k + 1)], A1[...], 0, 0).astype(BF)
        for b in range(2):
            e = 2 * k + b
            ro = jnp.zeros((1, D), F32)
            for i in range(n_e):
                ro = jnp.where(at_off(i) == e, g_router[i:i + 1, :], ro)
            foot = jnp.where(iota((16, D), 0) == 8, ro, 0.0).astype(BF)
            for d in range(4):
                cols = slice(128 * d, 128 * (d + 1))
                GG[d, brow(e, 0, part), :] = g2[part * b:part * (b + 1), cols]
                GG[d, brow(e, part, opart), :] = g_out[opart * e:opart * (e + 1), cols]
                GG[d, brow(e, part + opart, 16), :] = foot[:, cols]

    def rsc(k):
        d = dp_c if k == 0 else dp_cy
        return remote(GG.at[d], RCR.at[k], RSC, k, (dp_c, me))

    rsc(1).start()
    rsc(0).start()

    da1 = jnp.zeros((T, D), F32)
    for k in range(n_e // 2):
        da1 = da1 + dg(DQKV[:, 2 * part * k:2 * part * (k + 1)], qkv_weight(k), 1, 0)
    normed, inverse = norm_parts(XF[...])
    back, g_gain1, g_shift1 = norm_back(da1, normed, inverse, NRM[0:1])
    gtok = (DR[...] + back).astype(BF)
    grad_tok[...] = dg(move, gtok, 0, 0).astype(BF)
    row8 = iota((8, D), 0)
    stack = jnp.where(row8 == 0, g_gain1, jnp.where(row8 == 1, g_shift1, jnp.where(row8 == 2, g_gain2, jnp.where(row8 == 3, g_shift2, 0.0))))
    for k in range(D // 128):
        SM[0, k, 0:8, :] = stack[:, 128 * k:128 * (k + 1)]

    def smc(k):
        return remote(SM.at[k], SMCR.at[k], SMC, k, (dp_c if k == 0 else dp_y, me))

    def sm_join(a, b):
        is_sum = iota(a.shape, len(a.shape) - 2) < 8
        return jnp.where(is_sum, a + b, jnp.maximum(a, b))

    smc(0).start()
    rsc(1).wait_recv()
    RYS[...] = (GG[dp_y].astype(F32) + RCR[1].astype(F32)).astype(BF)
    rsy = remote(RYS, RYR, RSY, 0, (dp_y, me))
    rsy.start()
    smc(0).wait_recv()
    SM[1] = sm_join(SM[0], SMCR[0])
    smc(1).start()
    rsc(0).wait_recv()
    rsy.wait_recv()

    def rse(i, e):
        return remote(RES.at[brow(e)], RER.at[i], RSE, i, (dp, at_off(i)))

    def own_sum(e):
        at = brow(e)
        return GG[dp, at, :].astype(F32) + RCR[0, at, :].astype(F32) + RYR[at, :].astype(F32)

    for i in range(1, n_e):
        e = at_off(i)
        RES[brow(e), :] = own_sum(e).astype(BF)
        rse(i, e).start()
    smc(1).wait_recv()
    SM[2] = sm_join(SM[1], SMCR[1])

    def sme(i):
        return remote(SM.at[2, lax.div(at_off(i), 2)], SMER.at[i], SME, i, (dp, at_off(i)))

    for i in range(1, n_e):
        sme(i).start()
    dense = own_sum(me)
    for i in range(1, n_e):
        rse(i, at_off(i)).wait_recv()
        dense = dense + RER[i].astype(F32)
    tiny = SM[2, lax.div(me, 2)]
    for i in range(1, n_e):
        sme(i).wait_recv()
        tiny = sm_join(tiny, SMER[i])

    g_qkv = jnp.transpose(dense[0:part])
    grad_qkv[...] = g_qkv
    grad_out[...] = jnp.transpose(dense[part:part + opart])
    grad_router[...] = to_column(dense[part + opart + 8:part + opart + 9])
    grad_norm[...] = jnp.where(lax.rem(me, 2) == 0, tiny[0:4, 0:HEAD], tiny[0:4, HEAD:128])
    scale = jnp.sqrt(jnp.minimum(1.0, threshold[0].astype(F32) / tiny[8:16, :]))
    factors[...] = jnp.sum(jnp.where(iota((8, 128), 0) == iota((8, 128), 1), scale, 0.0), axis=0, keepdims=True)
    column = me * part + iota((1, part), 1)
    head = lax.rem(lax.div(column, HEAD), HEADS)
    scales = jnp.concatenate([scale, scale], axis=1)[:, :part]
    by_column = jnp.sum(jnp.where(iota((8, part), 0) == head, scales, 0.0), axis=0, keepdims=True)
    by_column = jnp.where(column < 2 * D, by_column, 1.0)
    clipped[...] = (w_qkv[...].astype(F32) - LEARN * g_qkv) * by_column

    for w, out in enumerate((grad_in, grad_down)):
        wgy(w).wait_recv()
        out[...] = out[...] + WYR[w].astype(F32)

    for i in range(1, n_e):
        to_token(SA, ZR, ZED, i).wait_recv()
    total = R[...] + dg(SELT[...], ZR[...], 1, 0)
    block_out[...] = dg(move, total.astype(BF), 0, 0).astype(BF)

    for i in range(1, n_e):
        dense_e(i, me, (dp, at_off(i))).wait_send()
        remote(GS.at[i], GR.at[i], GATE, i, (dp, at_off(i))).wait_send()
        to_token(SB, DXR, DXE, i).wait_send()
        to_token(SA, ZR, ZED, i).wait_send()
        remote(DGS.at[i], DGR.at[i], DGATE, i, (dp, from_off(i))).wait_send()
        rse(i, at_off(i)).wait_send()
        sme(i).wait_send()
    for i in range(n_e):
        dense_y(i).wait_send()
    for k in range(2):
        dense_c(k).wait_send()
        rsc(k).wait_send()
        smc(k).wait_send()
        wgy(k).wait_send()
        for w in range(2):
            wgc(k, w).wait_send()
    for k in range(6):
        exp_w(k).wait_send()
    rsy.wait_send()


def fused(tokens, w_qkv, w_out, w_router, norm_params, w_in, w_down, routes, threshold, cotangent):
    rows = tokens.shape[0]
    n_e = lax.axis_size("expert")
    images = rows // SEQ
    T = images * SEQP
    cap = 15 * routes.shape[1] * rows // (8 * n_e)
    cap = -(-cap // 16) * 16
    slots = n_e * cap
    part, opart = w_qkv.shape[1], w_out.shape[1]
    drows = w_qkv.shape[0]
    bundle = part + opart + 16
    ff = w_in.shape[2]
    V = pltpu.VMEM
    spec = pl.BlockSpec(memory_space=pltpu.VMEM)
    any_spec = pl.BlockSpec(memory_space=pl.ANY)
    S = jax.ShapeDtypeStruct
    outs = pl.pallas_call(
        functools.partial(block_kernel, n_e, cap, rows),
        out_shape=(
            S((rows, D), BF), S((rows, D), BF), S((drows, part), F32), S((drows, opart), F32), S((drows, 1), F32),
            S((4, HEAD), F32), S((D, ff), F32), S((ff, D), F32), S((drows, part), F32), S((1, 128), F32),
        ),
        in_specs=[spec] * 7 + [any_spec] * 2 + [pl.BlockSpec(memory_space=pltpu.SMEM)],
        out_specs=[spec] * 10,
        scratch_shapes=[
            V((4, n_e * bundle, 128), BF), V((4, D, ff), BF), V((4, ff, D), BF), V((T, D), F32), V((T, D), BF),
            V((T, D), F32), V((T, D), BF), V((T, D), BF), V((T, 3 * D), BF), V((T, D), BF),
            V((images * HEADS, SEQP, SEQP), F32), V((n_e, cap, T), BF), V((T, slots), BF), V((T, n_e), F32),
            V((16, D), F32), V((T, n_e), F32), V((n_e, D), BF),
            V((slots, D), BF), V((slots, D), BF), V((slots, D), BF), V((slots, D), BF), V((slots, D), BF), V((slots, D), BF),
            V((n_e, 8, cap), F32), V((n_e, 8, cap), F32), V((2 * cap, 1), F32), V((n_e, 8, cap), F32), V((n_e, 8, cap), F32),
            V((slots, 4 * ff), BF), V((slots, 4 * ff), BF), V((slots, D), BF),
            V((4, D, ff), BF), V((4, D, ff), BF), V((2, D, ff), BF), V((2, D, ff), BF),
            V((T, 3 * D), BF), V((T, D), BF), V((T, D), F32),
            V((4, n_e * bundle, 128), BF), V((2, n_e * bundle, 128), BF), V((n_e * bundle, 128), BF),
            V((n_e * bundle, 128), BF), V((n_e * bundle, 128), BF), V((n_e, bundle, 128), BF),
            V((3, D // 128, 16, 128), F32), V((2, D // 128, 16, 128), F32), V((n_e, 16, 128), F32),
            pltpu.SemaphoreType.DMA((17, 8)), pltpu.SemaphoreType.DMA((17, 8)), pltpu.SemaphoreType.DMA((2,)),
        ],
        compiler_params=pltpu.CompilerParams(
            collective_id=0, has_side_effects=True, vmem_limit_bytes=63 * 2 ** 20
        ),
    )(
        tokens, cotangent, routes, w_qkv, w_out, w_router, norm_params,
        w_in.reshape(D, ff), w_down.reshape(ff, D), threshold,
    )
    block_out, grad_tok, grad_qkv, grad_out, grad_router, grad_norm, grad_in, grad_down, clipped, factors = outs
    return (
        block_out, grad_tok, grad_qkv, grad_out, grad_router, grad_norm,
        grad_in[None], grad_down[None], clipped, factors[0, :HEADS],
    )


def layer_norm(values, norm_gain, norm_shift):
    center = jnp.mean(values, axis=-1, keepdims=True)
    centered = values - center
    inverse = lax.rsqrt(jnp.mean(centered * centered, axis=-1, keepdims=True) + EPS)
    normed = centered * inverse
    return (normed * norm_gain + norm_shift, normed, inverse)


def plain_norm_back(upstream, normed, inverse, norm_gain):
    scaled = upstream * norm_gain
    inner_term = (
        scaled
        - jnp.mean(scaled, axis=-1, keepdims=True)
        - normed * jnp.mean(scaled * normed, axis=-1, keepdims=True)
    )
    return (inverse * inner_term, jnp.sum(upstream * normed, axis=0), jnp.sum(upstream, axis=0))


def exact_gelu(inputs):
    return jax.nn.gelu(inputs, approximate=False)


def scores_of(queries, key_part):
    return jnp.einsum(
        "bqhd,bkhd->bhqk", queries, key_part, preferred_element_type=jnp.float32
    ) * HEAD ** (-0.5)


def contract_rows(left, right):
    return lax.dot_general(
        left, right, (((0,), (0,)), ((), ())), preferred_element_type=jnp.float32
    )


def contract_cols(left, right):
    return lax.dot_general(
        left, right, (((1,), (1,)), ((), ())), preferred_element_type=jnp.float32
    )


def fetch_forward(w_qkv, w_out, w_router, norm_params, w_in, w_down):
    col_parts = (
        lax.all_gather(w_qkv, "expert", axis=1, tiled=True),
        lax.all_gather(w_out, "expert", axis=1, tiled=True),
        lax.all_gather(w_router, "expert", axis=1, tiled=True),
        lax.all_gather(norm_params, "expert", axis=1, tiled=True),
    )
    full_parts = (
        lax.all_gather(col_parts[0], "dp", axis=0, tiled=True),
        lax.all_gather(col_parts[1], "dp", axis=0, tiled=True),
        lax.all_gather(col_parts[2], "dp", axis=0, tiled=True),
        lax.all_gather(w_in, "dp", axis=2, tiled=True),
        lax.all_gather(w_down, "dp", axis=1, tiled=True),
    )
    return (full_parts, col_parts[3])


def fetch_backward(w_qkv, w_out, w_router, w_in, w_down):
    col_parts = (
        lax.all_gather(w_qkv, "expert", axis=1, tiled=True),
        lax.all_gather(w_out, "expert", axis=1, tiled=True),
        lax.all_gather(w_router, "expert", axis=1, tiled=True),
    )
    return (
        lax.all_gather(col_parts[0], "dp", axis=0, tiled=True),
        lax.all_gather(col_parts[1], "dp", axis=0, tiled=True),
        lax.all_gather(col_parts[2], "dp", axis=0, tiled=True),
        lax.all_gather(w_in, "dp", axis=2, tiled=True),
        lax.all_gather(w_down, "dp", axis=1, tiled=True),
    )


def shards(tokens, w_qkv, w_out, w_router, norm_params, w_in, w_down, routes, threshold, cotangent):
    tok_count = tokens.shape[0]
    images = tok_count // SEQ
    experts = lax.axis_size("expert")
    top_count = routes.shape[1]
    capacity = 15 * top_count * tok_count // (8 * experts)
    full_parts, norm_gains = fetch_forward(w_qkv, w_out, w_router, norm_params, w_in, w_down)
    full_qkv, full_out, full_router, full_in, full_down = full_parts
    gain_rows = norm_gains.astype(jnp.float32)
    source = tokens.astype(jnp.float32)
    first_norm, normed_one, inverse_one = layer_norm(source, gain_rows[0], gain_rows[1])
    first_low = first_norm.astype(jnp.bfloat16)
    qkv_rows = jnp.dot(first_low, full_qkv, preferred_element_type=jnp.float32).astype(jnp.bfloat16)
    qkv_split = qkv_rows.reshape(images, SEQ, 3, HEADS, HEAD)
    queries, key_part, values = (qkv_split[:, :, 0], qkv_split[:, :, 1], qkv_split[:, :, 2])
    scores = scores_of(queries, key_part)
    head_peaks = jnp.max(scores, axis=(0, 2, 3))
    row_peak = jnp.max(scores, axis=-1, keepdims=True)
    log_total = row_peak + jnp.log(jnp.sum(jnp.exp(scores - row_peak), axis=-1, keepdims=True))
    probs_low = jnp.exp(scores - log_total).astype(jnp.bfloat16)
    attn_mixed = jnp.einsum(
        "bhqk,bkhd->bqhd", probs_low, values, preferred_element_type=jnp.float32
    )
    attn_mixed = attn_mixed.reshape(tok_count, D).astype(jnp.bfloat16)
    resid = source + jnp.dot(attn_mixed, full_out, preferred_element_type=jnp.float32)
    peak_logit = lax.pmax(head_peaks, ("dp", "expert"))
    second_norm, normed_two, inverse_two = layer_norm(resid, gain_rows[2], gain_rows[3])
    second_low = second_norm.astype(jnp.bfloat16)
    logits = jnp.dot(second_low, full_router, preferred_element_type=jnp.float32)
    router_probs = jax.nn.softmax(logits, axis=-1)
    expert_ids = jnp.arange(experts, dtype=jnp.int32)
    chosen = (routes[:, :, None] == expert_ids[None, None, :]).astype(jnp.float32)
    gate_weights = jnp.sum(chosen * router_probs[:, None, :], axis=-1)
    flat_routes = routes.reshape(-1)
    onehot = (flat_routes[:, None] == expert_ids[None, :]).astype(jnp.int32)
    count = flat_routes.shape[0]
    earlier = jnp.tril(jnp.ones((count, count), jnp.bfloat16), -1)
    before = jnp.dot(
        earlier, onehot.astype(jnp.bfloat16), preferred_element_type=jnp.float32
    ).astype(jnp.int32)
    target_slot = flat_routes * capacity + jnp.sum(before * onehot, axis=1)
    routed = jnp.repeat(second_low, top_count, axis=0)
    outgoing = jnp.zeros((experts * capacity, D), jnp.bfloat16).at[target_slot].set(routed)
    arrived = lax.all_to_all(
        outgoing.reshape(experts, capacity, D), "expert", split_axis=0, concat_axis=0, tiled=True
    )
    arrived = arrived.reshape(experts * capacity, D)
    hidden = jnp.dot(arrived, full_in[0], preferred_element_type=jnp.float32)
    active, gelu_back = jax.vjp(exact_gelu, hidden)
    active_low = active.astype(jnp.bfloat16)
    expert_out = jnp.dot(active_low, full_down[0], preferred_element_type=jnp.float32).astype(
        jnp.bfloat16
    )
    returned = lax.all_to_all(
        expert_out.reshape(experts, capacity, D), "expert", split_axis=0, concat_axis=0, tiled=True
    )
    picked = (
        returned.reshape(experts * capacity, D)[target_slot]
        .astype(jnp.float32)
        .reshape(tok_count, top_count, D)
    )
    output = resid + jnp.sum(picked * gate_weights[:, :, None], axis=1)
    upstream = cotangent.astype(jnp.float32)
    anchor, upstream = lax.optimization_barrier(((w_qkv, w_out, w_router, w_in, w_down), upstream))
    back_qkv, back_out, back_router, back_in, back_down = fetch_backward(
        anchor[0], anchor[1], anchor[2], anchor[3], anchor[4]
    )
    grad_picked = (
        (upstream[:, None, :] * gate_weights[:, :, None])
        .astype(jnp.bfloat16)
        .reshape(tok_count * top_count, D)
    )
    grad_gates = jnp.sum(upstream[:, None, :] * picked, axis=-1)
    grad_probs = jnp.sum(grad_gates[:, :, None] * chosen, axis=1)
    grad_logits = router_probs * (
        grad_probs - jnp.sum(grad_probs * router_probs, axis=-1, keepdims=True)
    )
    back_slots = jnp.zeros((experts * capacity, D), jnp.bfloat16).at[target_slot].set(grad_picked)
    grad_expert = lax.all_to_all(
        back_slots.reshape(experts, capacity, D), "expert", split_axis=0, concat_axis=0, tiled=True
    )
    grad_expert = grad_expert.reshape(experts * capacity, D)
    grad_down = contract_rows(active_low, grad_expert)
    grad_active = contract_cols(grad_expert, back_down[0])
    grad_hidden = gelu_back(grad_active)[0].astype(jnp.bfloat16)
    grad_in = contract_rows(arrived, grad_hidden)
    grad_rows = contract_cols(grad_hidden, back_in[0]).astype(jnp.bfloat16)
    grad_back = lax.all_to_all(
        grad_rows.reshape(experts, capacity, D), "expert", split_axis=0, concat_axis=0, tiled=True
    )
    grad_routed = grad_back.reshape(experts * capacity, D)[target_slot].astype(jnp.float32)
    router_float = back_router.astype(jnp.float32)
    grad_second = jnp.sum(grad_routed.reshape(tok_count, top_count, D), axis=1) + lax.dot_general(
        grad_logits, router_float, (((1,), (1,)), ((), ())), precision=lax.Precision.HIGHEST
    )
    grad_router = lax.dot_general(
        second_low.astype(jnp.float32),
        grad_logits,
        (((0,), (0,)), ((), ())),
        precision=lax.Precision.HIGHEST,
    )
    grad_resid_two, gain_two_grad, shift_two_grad = plain_norm_back(
        grad_second, normed_two, inverse_two, gain_rows[2]
    )
    grad_resid = upstream + grad_resid_two
    grad_resid_low = grad_resid.astype(jnp.bfloat16)
    grad_out = contract_rows(attn_mixed, grad_resid_low)
    grad_mixed = (
        contract_cols(grad_resid_low, back_out)
        .astype(jnp.bfloat16)
        .reshape(images, SEQ, HEADS, HEAD)
    )
    again_scores = scores_of(queries, key_part)
    probs_full = jnp.exp(again_scores - log_total)
    grad_attn = jnp.einsum(
        "bqhd,bkhd->bhqk", grad_mixed, values, preferred_element_type=jnp.float32
    )
    grad_scores = (
        probs_full * (grad_attn - jnp.sum(grad_attn * probs_full, axis=-1, keepdims=True))
    ).astype(jnp.bfloat16)
    grad_queries = jnp.einsum(
        "bhqk,bkhd->bqhd", grad_scores, key_part, preferred_element_type=jnp.float32
    ) * HEAD ** (-0.5)
    grad_keys = jnp.einsum(
        "bhqk,bqhd->bkhd", grad_scores, queries, preferred_element_type=jnp.float32
    ) * HEAD ** (-0.5)
    grad_values = jnp.einsum(
        "bhqk,bqhd->bkhd", probs_low, grad_mixed, preferred_element_type=jnp.float32
    )
    grad_qkv_rows = (
        jnp.stack([grad_queries, grad_keys, grad_values], axis=2)
        .reshape(tok_count, 3 * D)
        .astype(jnp.bfloat16)
    )
    grad_qkv = contract_rows(first_low, grad_qkv_rows)
    grad_first = contract_cols(grad_qkv_rows, back_qkv)
    grad_source, gain_one_grad, shift_one_grad = plain_norm_back(
        grad_first, normed_one, inverse_one, gain_rows[0]
    )
    grad_tokens = (grad_resid + grad_source).astype(jnp.bfloat16)
    norm_grads = jnp.stack([gain_one_grad, shift_one_grad, gain_two_grad, shift_two_grad])
    col_sums = (
        lax.psum_scatter(
            grad_qkv.astype(jnp.bfloat16), "expert", scatter_dimension=1, tiled=True
        ).astype(jnp.float32),
        lax.psum_scatter(
            grad_out.astype(jnp.bfloat16), "expert", scatter_dimension=1, tiled=True
        ).astype(jnp.float32),
        lax.psum_scatter(
            grad_router.astype(jnp.bfloat16), "expert", scatter_dimension=1, tiled=True
        ).astype(jnp.float32),
        lax.psum_scatter(
            norm_grads.astype(jnp.bfloat16), "expert", scatter_dimension=1, tiled=True
        ).astype(jnp.float32),
    )
    row_sums = (
        lax.psum_scatter(
            col_sums[0].astype(jnp.bfloat16), "dp", scatter_dimension=0, tiled=True
        ).astype(jnp.float32),
        lax.psum_scatter(
            col_sums[1].astype(jnp.bfloat16), "dp", scatter_dimension=0, tiled=True
        ).astype(jnp.float32),
        lax.psum_scatter(
            col_sums[2].astype(jnp.bfloat16), "dp", scatter_dimension=0, tiled=True
        ).astype(jnp.float32),
        lax.psum_scatter(
            grad_in[None].astype(jnp.bfloat16), "dp", scatter_dimension=2, tiled=True
        ).astype(jnp.float32),
        lax.psum_scatter(
            grad_down[None].astype(jnp.bfloat16), "dp", scatter_dimension=1, tiled=True
        ).astype(jnp.float32),
    )
    norm_total = lax.psum(col_sums[3], "dp")
    factors = jnp.sqrt(jnp.minimum(1.0, threshold[0].astype(jnp.float32) / peak_logit))
    col_width = w_qkv.shape[1]
    column = lax.axis_index("expert") * col_width + jnp.arange(col_width, dtype=jnp.int32)
    head_index = column % D // HEAD
    head_table = jnp.sum(
        jnp.where(
            head_index[:, None] == jnp.arange(HEADS, dtype=jnp.int32)[None, :],
            factors[None, :],
            0.0,
        ),
        axis=1,
    )
    column_scale = jnp.where(column < 2 * D, head_table, 1.0)
    clipped = (w_qkv.astype(jnp.float32) - LEARN * row_sums[0]) * column_scale[None, :]
    return (
        output.astype(jnp.bfloat16),
        grad_tokens,
        row_sums[0],
        row_sums[1],
        row_sums[2],
        norm_total,
        row_sums[3],
        row_sums[4],
        clipped,
        factors,
    )


def solution(mesh):
    in_specs = (
        P(("dp", "expert"), None),
        P("dp", "expert"),
        P("dp", "expert"),
        P("dp", "expert"),
        P(None, "expert"),
        P("expert", None, "dp"),
        P("expert", "dp", None),
        P(("dp", "expert"), None),
        P(),
        P(("dp", "expert"), None),
    )
    out_specs = (
        P(("dp", "expert"), None),
        P(("dp", "expert"), None),
        P("dp", "expert"),
        P("dp", "expert"),
        P("dp", "expert"),
        P(None, "expert"),
        P("expert", None, "dp"),
        P("expert", "dp", None),
        P("dp", "expert"),
        P(),
    )
    fits = mesh.shape["dp"] == 4 and mesh.shape["expert"] == 8
    return jax.shard_map(fused if fits else shards, mesh=mesh, in_specs=in_specs, out_specs=out_specs, check_vma=False)
```

```python
import functools

import jax
import jax.numpy as jnp
from jax import lax
from jax.experimental import pallas as pl
from jax.experimental.pallas import tpu as pltpu
from jax.sharding import PartitionSpec as P

D = 512
HEADS = 8
HEAD = 64
SEQ = 197
EPS = 1e-06
LEARN = 0.001
SEQP = 208
BF = jnp.bfloat16
F32 = jnp.float32
MESH = pl.DeviceIdType.MESH

(DENSE_Z, DENSE_X, DENSE_Y, DENSE_C, EXPW, CROSS, COT, ACT, GATE, DXE, ZED, DGATE, WGC, WGY, RSC, RSY, RSX, RSZ, SMC,
 SME) = range(20)


def dg(left, right, left_dim, right_dim):
    return lax.dot_general(
        left, right, (((left_dim,), (right_dim,)), ((), ())), preferred_element_type=F32
    )


def iota(shape, dim):
    return lax.broadcasted_iota(jnp.int32, shape, dim)


def eye(size, dtype=BF):
    return (iota((size, size), 0) == iota((size, size), 1)).astype(F32).astype(dtype)


def split_two(value):
    high = value.astype(BF)
    return high, (value - high.astype(F32)).astype(BF)


def to_row(column):
    size = column.shape[0]
    return jnp.sum(jnp.where(iota((size, size), 0) == iota((size, size), 1), column, 0.0), axis=0, keepdims=True)


def to_column(row):
    size = row.shape[1]
    return jnp.sum(jnp.where(iota((size, size), 0) == iota((size, size), 1), row, 0.0), axis=1, keepdims=True)


def norm_parts(values):
    centered = values - jnp.mean(values, axis=-1, keepdims=True)
    inverse = lax.rsqrt(jnp.mean(centered * centered, axis=-1, keepdims=True) + EPS)
    return centered * inverse, inverse


def norm_back(upstream, normed, inverse, gain):
    scaled = upstream * gain
    inner = scaled - jnp.mean(scaled, axis=-1, keepdims=True)
    inner = inner - normed * jnp.mean(scaled * normed, axis=-1, keepdims=True)
    return (
        inverse * inner,
        jnp.sum(upstream * normed, axis=0, keepdims=True),
        jnp.sum(upstream, axis=0, keepdims=True),
    )


def normal_parts(u):
    return 0.5 + 0.5 * lax.erf(u * 2.0 ** -0.5), u * (jnp.exp(-0.5 * u * u) * 0.3989422804014327)


def block_kernel(
    n_e, cap, rows,
    tok, cot, routes, w_qkv, w_out, w_router, norm, win, wdown, threshold,
    block_out, grad_tok, grad_qkv, grad_out, grad_router, grad_norm, grad_in, grad_down, clipped, factors,
    GB, WI, WD, XF, CP, R, A1, A2, QKV, O, PS, SEL, SELT, SLOT, NRM, PR, WR,
    SA, SB, CR, AR, ZR, DXR, GS, GR, GCOL, DGS, DGR, H, DU, DZ,
    WCS, WCR, WYR, DQKV, DR, GG, RCR, RYS, RYR, RXS, RXR, RZS, RZR, SM, SMCR, SMER,
    SLT, SLF, XC, XA, XDR, XZR,
    send, recv, local,
):
    dp = lax.axis_index("dp")
    me = lax.axis_index("expert")
    core = lax.rem(dp, 2)
    dp_c = dp + 1 - 2 * core
    dp_y = lax.rem(dp + 2, 4)
    dp_cy = lax.rem(dp_c + 2, 4)
    images = rows // SEQ
    T = images * SEQP
    part = 3 * D // n_e
    opart = D // n_e
    bundle = part + opart + 16

    half_n = n_e // 2
    group, place = lax.div(me, half_n), lax.rem(me, half_n)
    mirror = lax.rem(me + half_n, n_e)
    zz, xx = lax.div(me, 2), lax.rem(me, 2)
    z_n = n_e // 2

    def at_off(i):
        return lax.rem(me + i, n_e)

    def to_of(s):
        return lax.rem(group + s // half_n, 2) * half_n + lax.rem(place + s % half_n, half_n)

    def from_of(s):
        return lax.rem(group + s // half_n, 2) * half_n + lax.rem(place + half_n - s % half_n, half_n)

    def near(i):
        return group * half_n + lax.rem(place + i, half_n)

    def near_from(i):
        return group * half_n + lax.rem(place + half_n - i % half_n, half_n)

    def column(dz, other=0):
        return lax.rem(zz + z_n + dz, z_n) * 2 + lax.rem(xx + other, 2)

    pending = {}

    def remote(src, dst, kind, i, where):
        return pltpu.make_async_remote_copy(
            src_ref=src, dst_ref=dst, send_sem=send.at[kind, i], recv_sem=recv.at[kind, i],
            device_id=where, device_id_type=MESH,
        )

    def begin(kind, i, copy):
        pending[kind, i] = copy
        copy.start()

    def sent(kind, i):
        pending.pop((kind, i)).wait_send()

    def brow(e, start=0, size=None):
        return pl.ds(pl.multiple_of(bundle * e + start, 16), bundle if size is None else size)

    peers = [(dp, at_off(i)) for i in range(1, n_e)] + [(dp_y, me), (dp_c, me)]
    barrier = pltpu.get_barrier_semaphore()
    for p in peers:
        pl.semaphore_signal(barrier, inc=1, device_id=p, device_id_type=MESH)
    load_in = pltpu.make_async_copy(win, WI.at[dp], local.at[0])
    load_down = pltpu.make_async_copy(wdown, WD.at[dp], local.at[1])
    load_in.start()
    load_down.start()

    GB[dp, brow(me, 0, part), :] = w_qkv[...]
    GB[dp, brow(me, part, opart), :] = w_out[...]
    spread = (iota((16, 4), 0) == iota((16, 4), 1)).astype(F32).astype(BF)
    twice = (lax.rem(iota((HEAD, 128), 1), HEAD) == iota((HEAD, 128), 0)).astype(F32).astype(BF)
    small = dg(dg(spread, norm[...], 1, 0).astype(BF), twice, 1, 0)
    small = jnp.where(iota((16, 128), 0) == 8, w_router[...].astype(F32), small)
    GB[dp, brow(me, part + opart, 16), :] = small.astype(BF)

    move = ((lax.div(iota((T, rows), 0), SEQP) * SEQ + lax.rem(iota((T, rows), 0), SEQP) == iota((T, rows), 1))
            & (lax.rem(iota((T, rows), 0), SEQP) < SEQ)).astype(F32).astype(BF)
    CP[...] = dg(move, cot[...], 1, 0).astype(BF)
    XF[...] = dg(move, tok[...], 1, 0)
    pl.semaphore_wait(barrier, len(peers))

    def dense(kind, i, d, e, where):
        return remote(GB.at[d, brow(e)], GB.at[d, brow(e)], kind, i, where)

    def dense_z(dz, e):
        return dense(DENSE_Z, dz, dp, e, (dp, column(dz)))

    def dense_x(dz, e, d=dp):
        return dense(DENSE_X, dz, d, e, (dp, column(0, 1)))

    def dense_y(dz, e):
        return dense(DENSE_Y, dz, dp, e, (dp_y, me))

    def dense_c(i):
        d = dp if i == 0 else dp_y
        return remote(GB.at[d], GB.at[d], DENSE_C, i, (dp_c, me))

    for dz in (2, 1, 3):
        begin(DENSE_Z, dz, dense_z(dz, me))
    begin(DENSE_X, 0, dense_x(0, me))
    begin(DENSE_Y, 0, dense_y(0, me))

    which = routes[...]
    block = lax.rem(lax.rem(which, half_n) + half_n - place, half_n)
    away = jnp.where(lax.div(which, half_n) == group, block, block + half_n)
    named = (away[0:1] == iota((n_e, rows), 0)) | (away[1:2] == iota((n_e, rows), 0))
    named = named.astype(F32).astype(BF)
    chosen = dg(move, named, 1, 1)
    before = (iota((T, T), 1) < iota((T, T), 0)).astype(F32).astype(BF)
    chosen_low = chosen.astype(BF)
    slot = jnp.where(chosen > 0.5, dg(before, chosen_low, 1, 0), -1.0)
    SLOT[...] = slot
    chosen_t = dg(named, move, 1, 1)
    slot_t = jnp.where(chosen_t > 0.5, dg(chosen_t.astype(BF), before, 1, 1), -1.0)
    SLT[...] = slot_t
    slots_over = remote(SLT, SLF, CROSS, 0, (dp, mirror))
    cot_over = remote(CP, XC, CROSS, 1, (dp, mirror))
    lane = iota((T, 2 * cap), 1).astype(F32)
    level = iota((cap, T), 0).astype(F32)

    def choose(first, columns, rows_of):
        for k in range(half_n // 2):
            target = jnp.where(lane < cap, columns[:, 2 * k:2 * k + 1], columns[:, 2 * k + 1:2 * k + 2] + cap)
            at = cap * (first + 2 * k)
            SELT[:, at:at + 2 * cap] = (lane == target).astype(F32).astype(BF)
        for i in range(half_n):
            SEL[first + i] = (level == rows_of[i:i + 1, :]).astype(F32).astype(BF)

    choose(0, slot, slot_t)

    def pack(source, first, buf_s, buf_r, kind):
        for i in (2, 1, 3, 0):
            s = first + i
            packed = dg(SEL[s], source[...], 1, 0).astype(BF)
            if i == 0:
                buf_r[cap * s:cap * (s + 1)] = packed
            else:
                buf_s[cap * s:cap * (s + 1)] = packed
                begin(kind, s, near_copy(buf_s, buf_r, kind, s, near(i)))

    def near_copy(buf_s, buf_r, kind, s, e):
        return remote(buf_s.at[pl.ds(cap * s, cap)], buf_r.at[pl.ds(cap * s, cap)], kind, s, (dp, e))

    for dz in range(1, z_n):
        dense_z(dz, column(-dz)).wait_recv()
        begin(DENSE_X, dz, dense_x(dz, column(-dz)))
        begin(DENSE_Y, dz, dense_y(dz, column(-dz)))
    begin(CROSS, 0, slots_over)
    begin(CROSS, 1, cot_over)
    pack(CP, 0, SA, CR, COT)
    for dz in range(z_n):
        dense_x(dz, column(-dz, 1)).wait_recv()
        if dz < z_n // 2:
            begin(DENSE_Y, z_n + dz, dense_y(z_n + dz, column(-dz, 1)))
        dense_y(dz, column(-dz)).wait_recv()
        if dz >= z_n // 2:
            begin(DENSE_X, z_n + dz, dense_x(z_n + dz, column(-dz), dp_y))
    begin(DENSE_C, 0, dense_c(0))

    load_in.wait()
    load_down.wait()

    def exp_w(k):
        buf = WI if k % 2 == 0 else WD
        if k < 2:
            return remote(buf.at[dp], buf.at[dp], EXPW, k, (dp_y, me))
        d = dp if k < 4 else dp_y
        return remote(buf.at[d], buf.at[d], EXPW, k, (dp_c, me))

    for k in range(4):
        begin(EXPW, k, exp_w(k))

    half = iota((16, 128), 1) < HEAD
    pieces = []
    for k in range(D // 128):
        even = GB[dp, brow(2 * k, part + opart, 16), :].astype(F32)
        odd = GB[dp, brow(2 * k + 1, part + opart, 16), :].astype(F32)
        pieces.append(jnp.where(half, even, odd))
    NRM[...] = jnp.concatenate(pieces, axis=1)
    normed, _ = norm_parts(XF[...])
    A1[...] = (normed * NRM[0:1] + NRM[1:2]).astype(BF)

    for dz in range(z_n):
        if dz < z_n // 2:
            dense_y(z_n + dz, column(-dz, 1)).wait_recv()
        else:
            dense_x(z_n + dz, column(-dz, 1), dp_y).wait_recv()
    begin(DENSE_C, 1, dense_c(1))
    dense_c(0).wait_recv()
    dense_c(1).wait_recv()

    def dense_rows(e, start, size):
        return jnp.concatenate([GB[d, brow(e, start, size), :] for d in range(4)], axis=1)

    def qkv_weight(k):
        return jnp.concatenate([dense_rows(2 * k, 0, part), dense_rows(2 * k + 1, 0, part)], axis=0)

    def out_weight():
        return jnp.concatenate([dense_rows(e, part, opart) for e in range(n_e)], axis=0)

    for k in range(n_e // 2):
        QKV[:, 2 * part * k:2 * part * (k + 1)] = dg(A1[...], qkv_weight(k), 1, 1).astype(BF)

    slots_over.wait_recv()
    cot_over.wait_recv()
    slot_f = SLF[...]
    choose(half_n, dg(eye(T), slot_f[half_n:].astype(BF), 1, 1), slot_f[half_n:])
    pack(XC, half_n, SA, CR, COT)

    row_ok = iota((SEQP, SEQP), 0) < SEQ
    col_ok = iota((SEQP, SEQP), 1) < SEQ
    first_head = iota((1, 128), 1) < HEAD
    masks = [first_head.astype(F32).astype(BF), (~first_head).astype(F32).astype(BF)]

    def attend(g, peaks):
        img = lax.div(g, HEADS // 2)
        pair = lax.rem(g, HEADS // 2)
        at = pl.ds(pl.multiple_of(SEQP * img, 16), SEQP)
        q2 = QKV[at, pl.ds(pl.multiple_of(128 * pair, 128), 128)]
        k2 = QKV[at, pl.ds(pl.multiple_of(D + 128 * pair, 128), 128)]
        v2 = QKV[at, pl.ds(pl.multiple_of(2 * D + 128 * pair, 128), 128)]
        mixed = jnp.zeros((SEQP, 128), F32)
        for hh in range(2):
            s = dg(q2 * masks[hh], k2, 1, 1) * HEAD ** -0.5
            s = jnp.where(col_ok, s, -1e30)
            top = jnp.max(s, axis=1, keepdims=True)
            ex = jnp.exp(s - top)
            p = ex / jnp.sum(ex, axis=1, keepdims=True)
            PS[2 * g + hh] = p
            mixed = mixed + dg(p.astype(BF), v2 * masks[hh], 1, 0)
            peak = jnp.max(jnp.where(row_ok, s, -1e30), axis=(0, 1), keepdims=True)
            peaks = jnp.where(iota((8, 128), 0) == 2 * pair + hh, jnp.maximum(peaks, peak), peaks)
        O[at, pl.ds(pl.multiple_of(128 * pair, 128), 128)] = mixed.astype(BF)
        return peaks

    peaks = lax.fori_loop(0, images * HEADS // 2, attend, jnp.full((8, 128), -1e30, F32), unroll=True)
    for k in range(D // 128):
        SM[0, k, 8:16, :] = peaks

    for k in range(2):
        exp_w(k).wait_recv()
        begin(EXPW, 4 + k, exp_w(4 + k))

    R[...] = XF[...] + dg(O[...], out_weight(), 1, 1)
    normed, _ = norm_parts(R[...])
    A2[...] = (normed * NRM[2:3] + NRM[3:4]).astype(BF)
    act_over = remote(A2, XA, CROSS, 2, (dp, mirror))
    begin(CROSS, 2, act_over)
    pack(A2, 0, SB, AR, ACT)
    router = jnp.zeros((n_e, D), F32)
    for i in range(n_e):
        at = dense_rows(to_of(i), part + opart, 16).astype(F32)
        router = jnp.where(iota((n_e, D), 0) == i, at[8:9, :], router)
    WR[...] = router.astype(BF)
    logits = dg(A2[...], WR[...], 1, 1)
    ex = jnp.exp(logits - jnp.max(logits, axis=1, keepdims=True))
    PR[...] = ex / jnp.sum(ex, axis=1, keepdims=True)
    lane_cap = iota((T, cap), 1).astype(F32)

    def gate_copy(i):
        return remote(GS.at[i], GR.at[i], GATE, i, (dp, to_of(i)))

    for i in range(n_e):
        gate = SLOT[:, i:i + 1]
        gate = jnp.sum(jnp.where(lane_cap == gate, PR[:, i:i + 1], 0.0), axis=0, keepdims=True)
        if i == 0:
            GR[0] = jnp.broadcast_to(gate, (8, cap))
        else:
            GS[i] = jnp.broadcast_to(gate, (8, cap))
            begin(GATE, i, gate_copy(i))

    for k in range(2, 6):
        exp_w(k).wait_recv()

    pairs = n_e // 2

    def dgate_copy(i):
        return remote(DGS.at[i], DGR.at[i], DGATE, i, (dp, from_of(i)))

    act_over.wait_recv()
    pack(XA, half_n, SB, AR, ACT)
    for j in (0, 2, 3, 1):
        mine = pl.ds(2 * cap * j, 2 * cap)
        gates = []
        for i in (2 * j, 2 * j + 1):
            if i % half_n:
                near_copy(SA, CR, COT, i, near(i)).wait_recv()
                near_copy(SB, AR, ACT, i, near(i)).wait_recv()
                sent(COT, i)
                sent(ACT, i)
            if i > 0:
                gate_copy(i).wait_recv()
            gates.append(to_column(GR[i, 0:1, :]))
        gate = jnp.concatenate(gates, axis=0)
        GCOL[...] = gate
        DZ[mine] = (CR[mine].astype(F32) * gate).astype(BF)

        for q in range(8):
            d, at, to = q // 2, slice(256 * (q % 2), 256 * (q % 2) + 256), slice(256 * q, 256 * q + 256)
            u = dg(AR[mine], WI[d, :, at], 1, 0)
            dh = dg(CR[mine], WD[d, at, :], 1, 1)
            phi, slope = normal_parts(u)
            H[mine, to] = (u * phi).astype(BF)
            DU[mine, to] = (dh * (phi + slope) * GCOL[...]).astype(BF)
        z = dg(H[mine, :], WD[...].reshape(4 * 512, D), 1, 0)
        dx = dg(DU[mine, :], jnp.concatenate([WI[d] for d in range(4)], axis=1), 1, 1)
        z_low = z.astype(BF).astype(F32)
        dgate = jnp.sum(CR[mine].astype(F32) * z_low, axis=1, keepdims=True)
        z_out = (z_low * gate).astype(BF)
        dx_out = dx.astype(BF)
        for b, i in enumerate((2 * j, 2 * j + 1)):
            row = jnp.broadcast_to(to_row(dgate[cap * b:cap * (b + 1)]), (8, cap))
            at = slice(cap * i, cap * (i + 1))
            if i % half_n == 0:
                DXR[at] = dx_out[cap * b:cap * (b + 1)]
                ZR[at] = z_out[cap * b:cap * (b + 1)]
            else:
                SB[at] = dx_out[cap * b:cap * (b + 1)]
                SA[at] = z_out[cap * b:cap * (b + 1)]
                begin(DXE, i, near_copy(SB, DXR, DXE, i, near_from(i)))
            if i == 0:
                DGR[0] = row
            else:
                DGS[i] = row
                begin(DGATE, i, dgate_copy(i))

    mine = slice(0, cap * half_n)
    theirs = slice(cap * half_n, cap * n_e)

    def give_back(buf_r, kind, k, buf_s, over):
        for i in range(1, half_n):
            near_copy(SA, buf_r, kind, half_n + i, near_from(i)).wait_recv()
        buf_s[...] = dg(SELT[:, theirs], buf_r[theirs], 1, 0).astype(BF)
        begin(CROSS, k, over)

    sent_over = remote(XC, XDR, CROSS, 3, (dp, mirror))
    z_over = remote(XA, XZR, CROSS, 4, (dp, mirror))
    give_back(DXR, DXE, 3, XC, sent_over)
    def wg(d, w):
        at = pl.ds(pl.multiple_of(512 * d, 512), 512)
        if w == 0:
            return dg(AR[...], DU[:, at], 0, 0)
        return dg(H[:, at], DZ[...], 0, 0)

    yy = lax.div(dp, 2)
    def wgc(jy, w):
        return remote(WCS.at[2 * jy + w], WCR.at[2 * jy + w], WGC, 2 * jy + w, (dp_c, me))

    def wgy(w):
        return remote(WCS.at[2 + w], WYR.at[w], WGY, w, (dp_y, me))

    for jy in (1, 0):
        for w in range(2):
            WCS[2 * jy + w] = wg(lax.rem(yy + jy, 2) * 2 + 1 - core, w).astype(BF)
            begin(WGC, 2 * jy + w, wgc(jy, w))
    for i in (5, 6, 7, 1, 2, 3):
        begin(ZED, i, near_copy(SA, ZR, ZED, i, near_from(i)))
    for w in range(2):
        total = wg(dp_y, w)
        wgc(1, w).wait_recv()
        sent(WGC, 2 + w)
        WCS[2 + w] = (total + WCR[2 + w].astype(F32)).astype(BF)
        begin(WGY, w, wgy(w))
    for w, out in enumerate((grad_in, grad_down)):
        total = wg(dp, w)
        wgc(0, w).wait_recv()
        out[...] = total + WCR[w].astype(F32)

    for i in range(1, n_e):
        dgate_copy(i).wait_recv()
        if i < half_n:
            near_copy(SB, DXR, DXE, i, near_from(i)).wait_recv()
    sent_over.wait_recv()
    lane_e = iota((T, n_e), 1)
    dprob = jnp.zeros((T, n_e), F32)
    for i in range(n_e):
        got = jnp.sum(jnp.where(lane_cap == SLOT[:, i:i + 1], DGR[i, 0:1, :], 0.0), axis=1, keepdims=True)
        dprob = jnp.where(lane_e == i, got, dprob)
    prob = PR[...]
    dlogit = prob * (dprob - jnp.sum(dprob * prob, axis=1, keepdims=True))
    high, low = split_two(dlogit)
    da2 = dg(SELT[:, mine], DXR[mine], 1, 0) + XDR[...].astype(F32)
    da2 = da2 + dg(high, WR[...], 1, 0) + dg(low, WR[...], 1, 0)
    g_router = dg(high, A2[...], 0, 0) + dg(low, A2[...], 0, 0)
    normed, inverse = norm_parts(R[...])
    back, g_gain2, g_shift2 = norm_back(da2, normed, inverse, NRM[2:3])
    DR[...] = CP[...].astype(F32) + back
    dy = DR[...].astype(BF)
    sent(CROSS, 1)
    DO = CP
    DO[...] = dg(dy, out_weight(), 1, 0).astype(BF)
    g_out = dg(dy, O[...], 0, 0).astype(BF)

    def attend_back(g, carry):
        img = lax.div(g, HEADS // 2)
        pair = lax.rem(g, HEADS // 2)
        at = pl.ds(pl.multiple_of(SEQP * img, 16), SEQP)
        cq = pl.ds(pl.multiple_of(128 * pair, 128), 128)
        ck = pl.ds(pl.multiple_of(D + 128 * pair, 128), 128)
        cv = pl.ds(pl.multiple_of(2 * D + 128 * pair, 128), 128)
        q2, k2, v2, do2 = QKV[at, cq], QKV[at, ck], QKV[at, cv], DO[at, cq]
        dq = dk = dv = jnp.zeros((SEQP, 128), F32)
        for hh in range(2):
            p = PS[2 * g + hh]
            do_h = do2 * masks[hh]
            dpr = dg(do_h, v2, 1, 1)
            ds = (p * (dpr - jnp.sum(dpr * p, axis=1, keepdims=True))).astype(BF)
            dq = dq + dg(ds, k2 * masks[hh], 1, 0)
            dk = dk + dg(ds, q2 * masks[hh], 0, 0)
            dv = dv + dg(p.astype(BF), do_h, 0, 0)
        DQKV[at, cq] = (dq * HEAD ** -0.5).astype(BF)
        DQKV[at, ck] = (dk * HEAD ** -0.5).astype(BF)
        DQKV[at, cv] = dv.astype(BF)
        return carry

    lax.fori_loop(0, images * HEADS // 2, attend_back, 0, unroll=True)

    give_back(ZR, ZED, 4, XA, z_over)

    for k in range(n_e // 2):
        g2 = dg(DQKV[:, 2 * part * k:2 * part * (k + 1)], A1[...], 0, 0).astype(BF)
        for b in range(2):
            e = 2 * k + b
            ro = jnp.zeros((1, D), F32)
            for i in range(n_e):
                ro = jnp.where(to_of(i) == e, g_router[i:i + 1, :], ro)
            foot = jnp.where(iota((16, D), 0) == 8, ro, 0.0).astype(BF)
            for d in range(4):
                cols = slice(128 * d, 128 * (d + 1))
                GG[d, brow(e, 0, part), :] = g2[part * b:part * (b + 1), cols]
                GG[d, brow(e, part, opart), :] = g_out[opart * e:opart * (e + 1), cols]
                GG[d, brow(e, part + opart, 16), :] = foot[:, cols]

    def rsc(k):
        d = dp_c if k == 0 else dp_cy
        return remote(GG.at[d], RCR.at[k], RSC, k, (dp_c, me))

    begin(RSC, 1, rsc(1))
    begin(RSC, 0, rsc(0))

    da1 = jnp.zeros((T, D), F32)
    for k in range(n_e // 2):
        da1 = da1 + dg(DQKV[:, 2 * part * k:2 * part * (k + 1)], qkv_weight(k), 1, 0)
    normed, inverse = norm_parts(XF[...])
    back, g_gain1, g_shift1 = norm_back(da1, normed, inverse, NRM[0:1])
    gtok = (DR[...] + back).astype(BF)
    grad_tok[...] = dg(move, gtok, 0, 0).astype(BF)
    row8 = iota((8, D), 0)
    stack = jnp.where(row8 == 0, g_gain1, jnp.where(row8 == 1, g_shift1, jnp.where(row8 == 2, g_gain2, jnp.where(row8 == 3, g_shift2, 0.0))))
    for k in range(D // 128):
        SM[0, k, 0:8, :] = stack[:, 128 * k:128 * (k + 1)]

    def smc(k):
        return remote(SM.at[k], SMCR.at[k], SMC, k, (dp_c if k == 0 else dp_y, me))

    def sm_join(a, b):
        is_sum = iota(a.shape, len(a.shape) - 2) < 8
        return jnp.where(is_sum, a + b, jnp.maximum(a, b))

    begin(SMC, 0, smc(0))
    rsc(1).wait_recv()

    def rsy(i, e):
        return remote(RYS.at[brow(e)], RYR.at[brow(e)], RSY, i, (dp_y, me))

    order = [(dz, other) for other in (1, 0) for dz in (1, 2, 3, 0)]
    for i, (dz, other) in enumerate(order):
        at = brow(column(dz, other))
        RYS[at, :] = (GG[dp_y, at, :].astype(F32) + RCR[1, at, :].astype(F32)).astype(BF)
        begin(RSY, i, rsy(i, column(dz, other)))
    smc(0).wait_recv()
    SM[1] = sm_join(SM[0], SMCR[0])
    begin(SMC, 1, smc(1))
    rsc(0).wait_recv()

    def rsx(dz):
        return remote(RXS.at[dz], RXR.at[dz], RSX, dz, (dp, column(0, 1)))

    def rsz(dz):
        return remote(RZS.at[dz], RZR.at[dz], RSZ, dz, (dp, column(dz)))

    def own_sum(i, dz, other):
        at = brow(column(dz, other))
        rsy(i, column(dz, other)).wait_recv()
        return GG[dp, at, :].astype(F32) + RCR[0, at, :].astype(F32) + RYR[at, :].astype(F32)

    dense_sum = None
    for i, (dz, other) in enumerate(order):
        total = own_sum(i, dz, other)
        if other:
            RXS[dz] = total.astype(BF)
            begin(RSX, dz, rsx(dz))
            continue
        rsx(dz).wait_recv()
        total = total + RXR[dz].astype(F32)
        if dz:
            RZS[dz] = total.astype(BF)
            begin(RSZ, dz, rsz(dz))
        else:
            dense_sum = total
    smc(1).wait_recv()
    SM[2] = sm_join(SM[1], SMCR[1])

    def sme(i):
        return remote(SM.at[2, lax.div(at_off(i), 2)], SMER.at[i], SME, i, (dp, at_off(i)))

    for i in range(1, n_e):
        begin(SME, i, sme(i))
    for dz in range(1, z_n):
        rsz(dz).wait_recv()
        dense_sum = dense_sum + RZR[dz].astype(F32)
    tiny = SM[2, lax.div(me, 2)]
    for i in range(1, n_e):
        sme(i).wait_recv()
        tiny = sm_join(tiny, SMER[i])

    g_qkv = dense_sum[0:part]
    grad_qkv[...] = g_qkv
    grad_out[...] = dense_sum[part:part + opart]
    grad_router[...] = dense_sum[part + opart + 8:part + opart + 9]
    grad_norm[...] = jnp.where(lax.rem(me, 2) == 0, tiny[0:4, 0:HEAD], tiny[0:4, HEAD:128])
    scale = jnp.sqrt(jnp.minimum(1.0, threshold[0].astype(F32) / tiny[8:16, :]))
    diagonal = jnp.where(iota((8, 128), 0) == iota((8, 128), 1), scale, 0.0)
    factors[...] = jnp.sum(diagonal, axis=0, keepdims=True)[:, 0:HEADS]
    column = me * part + iota((part, 128), 0)
    head = jnp.where(column < 2 * D, lax.rem(lax.div(column, HEAD), HEADS), HEADS)
    by_column = jnp.ones((part, 128), F32)
    for h in range(HEADS):
        by_column = jnp.where(head == h, scale[h:h + 1, :], by_column)
    clipped[...] = (w_qkv[...].astype(F32) - LEARN * g_qkv) * by_column

    for w, out in enumerate((grad_in, grad_down)):
        wgy(w).wait_recv()
        out[...] = out[...] + WYR[w].astype(F32)

    for i in range(1, half_n):
        near_copy(SA, ZR, ZED, i, near_from(i)).wait_recv()
    z_over.wait_recv()
    total = R[...] + dg(SELT[:, mine], ZR[mine], 1, 0) + XZR[...].astype(F32)
    block_out[...] = dg(move, total.astype(BF), 0, 0).astype(BF)

    for kind, i in list(pending):
        sent(kind, i)


def deliver(*refs):
    spots = len(refs) // 2
    done = refs[-1]
    copies = [pltpu.make_async_copy(refs[i], refs[spots + i], done.at[i]) for i in range(spots)]
    for copy in copies:
        copy.start()
    for copy in copies:
        copy.wait()


def fused(tokens, w_qkv, w_out, w_router, norm_params, w_in, w_down, routes, threshold, cotangent):
    rows = tokens.shape[0]
    n_e = lax.axis_size("expert")
    images = rows // SEQ
    T = images * SEQP
    cap = 15 * routes.shape[1] * rows // (8 * n_e)
    cap = -(-cap // 16) * 16
    slots = n_e * cap
    part, opart = w_qkv.shape[1], w_out.shape[1]
    drows = w_qkv.shape[0]
    bundle = part + opart + 16
    ff = w_in.shape[2]
    V = pltpu.VMEM
    spec = pl.BlockSpec(memory_space=pltpu.VMEM)
    any_spec = pl.BlockSpec(memory_space=pl.ANY)
    S = jax.ShapeDtypeStruct
    outs = pl.pallas_call(
        functools.partial(block_kernel, n_e, cap, rows),
        out_shape=(
            S((rows, D), BF), S((rows, D), BF), S((part, drows), F32), S((opart, drows), F32), S((1, drows), F32),
            S((4, HEAD), F32), S((D, ff), F32), S((ff, D), F32), S((part, drows), F32), S((1, HEADS), F32),
        ),
        in_specs=[spec] * 7 + [any_spec] * 2 + [pl.BlockSpec(memory_space=pltpu.SMEM)],
        out_specs=[spec] * 10,
        scratch_shapes=[
            V((4, n_e * bundle, 128), BF), V((4, D, ff), BF), V((4, ff, D), BF), V((T, D), F32), V((T, D), BF),
            V((T, D), F32), V((T, D), BF), V((T, D), BF), V((T, 3 * D), BF), V((T, D), BF),
            V((images * HEADS, SEQP, SEQP), F32), V((n_e, cap, T), BF), V((T, slots), BF), V((T, n_e), F32),
            V((16, D), F32), V((T, n_e), F32), V((n_e, D), BF),
            V((slots, D), BF), V((slots, D), BF), V((slots, D), BF), V((slots, D), BF), V((slots, D), BF), V((slots, D), BF),
            V((n_e, 8, cap), F32), V((n_e, 8, cap), F32), V((2 * cap, 1), F32), V((n_e, 8, cap), F32), V((n_e, 8, cap), F32),
            V((slots, 4 * ff), BF), V((slots, 4 * ff), BF), V((slots, D), BF),
            V((4, D, ff), BF), V((4, D, ff), BF), V((2, D, ff), BF),
            V((T, 3 * D), BF), V((T, D), F32),
            V((4, n_e * bundle, 128), BF), V((2, n_e * bundle, 128), BF), V((n_e * bundle, 128), BF),
            V((n_e * bundle, 128), BF), V((n_e // 2, bundle, 128), BF), V((n_e // 2, bundle, 128), BF),
            V((n_e // 2, bundle, 128), BF), V((n_e // 2, bundle, 128), BF),
            V((3, D // 128, 16, 128), F32), V((2, D // 128, 16, 128), F32), V((n_e, 16, 128), F32),
            V((n_e, T), F32), V((n_e, T), F32), V((T, D), BF), V((T, D), BF), V((T, D), BF), V((T, D), BF),
            pltpu.SemaphoreType.DMA((20, 8)), pltpu.SemaphoreType.DMA((20, 8)), pltpu.SemaphoreType.DMA((2,)),
        ],
        compiler_params=pltpu.CompilerParams(
            collective_id=0, has_side_effects=True, vmem_limit_bytes=63 * 2 ** 20
        ),
    )(
        tokens, cotangent, routes.T, w_qkv.T, w_out.T, w_router.T, norm_params,
        w_in.reshape(D, ff), w_down.reshape(ff, D), threshold,
    )
    spots = len(outs)
    outs = pl.pallas_call(
        deliver,
        out_shape=tuple(S(o.shape, o.dtype) for o in outs),
        in_specs=[spec] * spots,
        out_specs=[any_spec] * spots,
        scratch_shapes=[pltpu.SemaphoreType.DMA((spots,))],
    )(*outs)
    block_out, grad_tok, grad_qkv, grad_out, grad_router, grad_norm, grad_in, grad_down, clipped, factors = outs
    return (
        block_out, grad_tok, grad_qkv.T, grad_out.T, grad_router.T, grad_norm,
        grad_in[None], grad_down[None], clipped.T, factors.reshape(HEADS),
    )


def layer_norm(values, norm_gain, norm_shift):
    center = jnp.mean(values, axis=-1, keepdims=True)
    centered = values - center
    inverse = lax.rsqrt(jnp.mean(centered * centered, axis=-1, keepdims=True) + EPS)
    normed = centered * inverse
    return (normed * norm_gain + norm_shift, normed, inverse)


def plain_norm_back(upstream, normed, inverse, norm_gain):
    scaled = upstream * norm_gain
    inner_term = (
        scaled
        - jnp.mean(scaled, axis=-1, keepdims=True)
        - normed * jnp.mean(scaled * normed, axis=-1, keepdims=True)
    )
    return (inverse * inner_term, jnp.sum(upstream * normed, axis=0), jnp.sum(upstream, axis=0))


def exact_gelu(inputs):
    return jax.nn.gelu(inputs, approximate=False)


def scores_of(queries, key_part):
    return jnp.einsum(
        "bqhd,bkhd->bhqk", queries, key_part, preferred_element_type=jnp.float32
    ) * HEAD ** (-0.5)


def contract_rows(left, right):
    return lax.dot_general(
        left, right, (((0,), (0,)), ((), ())), preferred_element_type=jnp.float32
    )


def contract_cols(left, right):
    return lax.dot_general(
        left, right, (((1,), (1,)), ((), ())), preferred_element_type=jnp.float32
    )


def fetch_forward(w_qkv, w_out, w_router, norm_params, w_in, w_down):
    col_parts = (
        lax.all_gather(w_qkv, "expert", axis=1, tiled=True),
        lax.all_gather(w_out, "expert", axis=1, tiled=True),
        lax.all_gather(w_router, "expert", axis=1, tiled=True),
        lax.all_gather(norm_params, "expert", axis=1, tiled=True),
    )
    full_parts = (
        lax.all_gather(col_parts[0], "dp", axis=0, tiled=True),
        lax.all_gather(col_parts[1], "dp", axis=0, tiled=True),
        lax.all_gather(col_parts[2], "dp", axis=0, tiled=True),
        lax.all_gather(w_in, "dp", axis=2, tiled=True),
        lax.all_gather(w_down, "dp", axis=1, tiled=True),
    )
    return (full_parts, col_parts[3])


def fetch_backward(w_qkv, w_out, w_router, w_in, w_down):
    col_parts = (
        lax.all_gather(w_qkv, "expert", axis=1, tiled=True),
        lax.all_gather(w_out, "expert", axis=1, tiled=True),
        lax.all_gather(w_router, "expert", axis=1, tiled=True),
    )
    return (
        lax.all_gather(col_parts[0], "dp", axis=0, tiled=True),
        lax.all_gather(col_parts[1], "dp", axis=0, tiled=True),
        lax.all_gather(col_parts[2], "dp", axis=0, tiled=True),
        lax.all_gather(w_in, "dp", axis=2, tiled=True),
        lax.all_gather(w_down, "dp", axis=1, tiled=True),
    )


def shards(tokens, w_qkv, w_out, w_router, norm_params, w_in, w_down, routes, threshold, cotangent):
    tok_count = tokens.shape[0]
    images = tok_count // SEQ
    experts = lax.axis_size("expert")
    top_count = routes.shape[1]
    capacity = 15 * top_count * tok_count // (8 * experts)
    full_parts, norm_gains = fetch_forward(w_qkv, w_out, w_router, norm_params, w_in, w_down)
    full_qkv, full_out, full_router, full_in, full_down = full_parts
    gain_rows = norm_gains.astype(jnp.float32)
    source = tokens.astype(jnp.float32)
    first_norm, normed_one, inverse_one = layer_norm(source, gain_rows[0], gain_rows[1])
    first_low = first_norm.astype(jnp.bfloat16)
    qkv_rows = jnp.dot(first_low, full_qkv, preferred_element_type=jnp.float32).astype(jnp.bfloat16)
    qkv_split = qkv_rows.reshape(images, SEQ, 3, HEADS, HEAD)
    queries, key_part, values = (qkv_split[:, :, 0], qkv_split[:, :, 1], qkv_split[:, :, 2])
    scores = scores_of(queries, key_part)
    head_peaks = jnp.max(scores, axis=(0, 2, 3))
    row_peak = jnp.max(scores, axis=-1, keepdims=True)
    log_total = row_peak + jnp.log(jnp.sum(jnp.exp(scores - row_peak), axis=-1, keepdims=True))
    probs_low = jnp.exp(scores - log_total).astype(jnp.bfloat16)
    attn_mixed = jnp.einsum(
        "bhqk,bkhd->bqhd", probs_low, values, preferred_element_type=jnp.float32
    )
    attn_mixed = attn_mixed.reshape(tok_count, D).astype(jnp.bfloat16)
    resid = source + jnp.dot(attn_mixed, full_out, preferred_element_type=jnp.float32)
    peak_logit = lax.pmax(head_peaks, ("dp", "expert"))
    second_norm, normed_two, inverse_two = layer_norm(resid, gain_rows[2], gain_rows[3])
    second_low = second_norm.astype(jnp.bfloat16)
    logits = jnp.dot(second_low, full_router, preferred_element_type=jnp.float32)
    router_probs = jax.nn.softmax(logits, axis=-1)
    expert_ids = jnp.arange(experts, dtype=jnp.int32)
    chosen = (routes[:, :, None] == expert_ids[None, None, :]).astype(jnp.float32)
    gate_weights = jnp.sum(chosen * router_probs[:, None, :], axis=-1)
    flat_routes = routes.reshape(-1)
    onehot = (flat_routes[:, None] == expert_ids[None, :]).astype(jnp.int32)
    count = flat_routes.shape[0]
    earlier = jnp.tril(jnp.ones((count, count), jnp.bfloat16), -1)
    before = jnp.dot(
        earlier, onehot.astype(jnp.bfloat16), preferred_element_type=jnp.float32
    ).astype(jnp.int32)
    target_slot = flat_routes * capacity + jnp.sum(before * onehot, axis=1)
    routed = jnp.repeat(second_low, top_count, axis=0)
    outgoing = jnp.zeros((experts * capacity, D), jnp.bfloat16).at[target_slot].set(routed)
    arrived = lax.all_to_all(
        outgoing.reshape(experts, capacity, D), "expert", split_axis=0, concat_axis=0, tiled=True
    )
    arrived = arrived.reshape(experts * capacity, D)
    hidden = jnp.dot(arrived, full_in[0], preferred_element_type=jnp.float32)
    active, gelu_back = jax.vjp(exact_gelu, hidden)
    active_low = active.astype(jnp.bfloat16)
    expert_out = jnp.dot(active_low, full_down[0], preferred_element_type=jnp.float32).astype(
        jnp.bfloat16
    )
    returned = lax.all_to_all(
        expert_out.reshape(experts, capacity, D), "expert", split_axis=0, concat_axis=0, tiled=True
    )
    picked = (
        returned.reshape(experts * capacity, D)[target_slot]
        .astype(jnp.float32)
        .reshape(tok_count, top_count, D)
    )
    output = resid + jnp.sum(picked * gate_weights[:, :, None], axis=1)
    upstream = cotangent.astype(jnp.float32)
    anchor, upstream = lax.optimization_barrier(((w_qkv, w_out, w_router, w_in, w_down), upstream))
    back_qkv, back_out, back_router, back_in, back_down = fetch_backward(
        anchor[0], anchor[1], anchor[2], anchor[3], anchor[4]
    )
    grad_picked = (
        (upstream[:, None, :] * gate_weights[:, :, None])
        .astype(jnp.bfloat16)
        .reshape(tok_count * top_count, D)
    )
    grad_gates = jnp.sum(upstream[:, None, :] * picked, axis=-1)
    grad_probs = jnp.sum(grad_gates[:, :, None] * chosen, axis=1)
    grad_logits = router_probs * (
        grad_probs - jnp.sum(grad_probs * router_probs, axis=-1, keepdims=True)
    )
    back_slots = jnp.zeros((experts * capacity, D), jnp.bfloat16).at[target_slot].set(grad_picked)
    grad_expert = lax.all_to_all(
        back_slots.reshape(experts, capacity, D), "expert", split_axis=0, concat_axis=0, tiled=True
    )
    grad_expert = grad_expert.reshape(experts * capacity, D)
    grad_down = contract_rows(active_low, grad_expert)
    grad_active = contract_cols(grad_expert, back_down[0])
    grad_hidden = gelu_back(grad_active)[0].astype(jnp.bfloat16)
    grad_in = contract_rows(arrived, grad_hidden)
    grad_rows = contract_cols(grad_hidden, back_in[0]).astype(jnp.bfloat16)
    grad_back = lax.all_to_all(
        grad_rows.reshape(experts, capacity, D), "expert", split_axis=0, concat_axis=0, tiled=True
    )
    grad_routed = grad_back.reshape(experts * capacity, D)[target_slot].astype(jnp.float32)
    router_float = back_router.astype(jnp.float32)
    grad_second = jnp.sum(grad_routed.reshape(tok_count, top_count, D), axis=1) + lax.dot_general(
        grad_logits, router_float, (((1,), (1,)), ((), ())), precision=lax.Precision.HIGHEST
    )
    grad_router = lax.dot_general(
        second_low.astype(jnp.float32),
        grad_logits,
        (((0,), (0,)), ((), ())),
        precision=lax.Precision.HIGHEST,
    )
    grad_resid_two, gain_two_grad, shift_two_grad = plain_norm_back(
        grad_second, normed_two, inverse_two, gain_rows[2]
    )
    grad_resid = upstream + grad_resid_two
    grad_resid_low = grad_resid.astype(jnp.bfloat16)
    grad_out = contract_rows(attn_mixed, grad_resid_low)
    grad_mixed = (
        contract_cols(grad_resid_low, back_out)
        .astype(jnp.bfloat16)
        .reshape(images, SEQ, HEADS, HEAD)
    )
    again_scores = scores_of(queries, key_part)
    probs_full = jnp.exp(again_scores - log_total)
    grad_attn = jnp.einsum(
        "bqhd,bkhd->bhqk", grad_mixed, values, preferred_element_type=jnp.float32
    )
    grad_scores = (
        probs_full * (grad_attn - jnp.sum(grad_attn * probs_full, axis=-1, keepdims=True))
    ).astype(jnp.bfloat16)
    grad_queries = jnp.einsum(
        "bhqk,bkhd->bqhd", grad_scores, key_part, preferred_element_type=jnp.float32
    ) * HEAD ** (-0.5)
    grad_keys = jnp.einsum(
        "bhqk,bqhd->bkhd", grad_scores, queries, preferred_element_type=jnp.float32
    ) * HEAD ** (-0.5)
    grad_values = jnp.einsum(
        "bhqk,bqhd->bkhd", probs_low, grad_mixed, preferred_element_type=jnp.float32
    )
    grad_qkv_rows = (
        jnp.stack([grad_queries, grad_keys, grad_values], axis=2)
        .reshape(tok_count, 3 * D)
        .astype(jnp.bfloat16)
    )
    grad_qkv = contract_rows(first_low, grad_qkv_rows)
    grad_first = contract_cols(grad_qkv_rows, back_qkv)
    grad_source, gain_one_grad, shift_one_grad = plain_norm_back(
        grad_first, normed_one, inverse_one, gain_rows[0]
    )
    grad_tokens = (grad_resid + grad_source).astype(jnp.bfloat16)
    norm_grads = jnp.stack([gain_one_grad, shift_one_grad, gain_two_grad, shift_two_grad])
    col_sums = (
        lax.psum_scatter(
            grad_qkv.astype(jnp.bfloat16), "expert", scatter_dimension=1, tiled=True
        ).astype(jnp.float32),
        lax.psum_scatter(
            grad_out.astype(jnp.bfloat16), "expert", scatter_dimension=1, tiled=True
        ).astype(jnp.float32),
        lax.psum_scatter(
            grad_router.astype(jnp.bfloat16), "expert", scatter_dimension=1, tiled=True
        ).astype(jnp.float32),
        lax.psum_scatter(
            norm_grads.astype(jnp.bfloat16), "expert", scatter_dimension=1, tiled=True
        ).astype(jnp.float32),
    )
    row_sums = (
        lax.psum_scatter(
            col_sums[0].astype(jnp.bfloat16), "dp", scatter_dimension=0, tiled=True
        ).astype(jnp.float32),
        lax.psum_scatter(
            col_sums[1].astype(jnp.bfloat16), "dp", scatter_dimension=0, tiled=True
        ).astype(jnp.float32),
        lax.psum_scatter(
            col_sums[2].astype(jnp.bfloat16), "dp", scatter_dimension=0, tiled=True
        ).astype(jnp.float32),
        lax.psum_scatter(
            grad_in[None].astype(jnp.bfloat16), "dp", scatter_dimension=2, tiled=True
        ).astype(jnp.float32),
        lax.psum_scatter(
            grad_down[None].astype(jnp.bfloat16), "dp", scatter_dimension=1, tiled=True
        ).astype(jnp.float32),
    )
    norm_total = lax.psum(col_sums[3], "dp")
    factors = jnp.sqrt(jnp.minimum(1.0, threshold[0].astype(jnp.float32) / peak_logit))
    col_width = w_qkv.shape[1]
    column = lax.axis_index("expert") * col_width + jnp.arange(col_width, dtype=jnp.int32)
    head_index = column % D // HEAD
    head_table = jnp.sum(
        jnp.where(
            head_index[:, None] == jnp.arange(HEADS, dtype=jnp.int32)[None, :],
            factors[None, :],
            0.0,
        ),
        axis=1,
    )
    column_scale = jnp.where(column < 2 * D, head_table, 1.0)
    clipped = (w_qkv.astype(jnp.float32) - LEARN * row_sums[0]) * column_scale[None, :]
    return (
        output.astype(jnp.bfloat16),
        grad_tokens,
        row_sums[0],
        row_sums[1],
        row_sums[2],
        norm_total,
        row_sums[3],
        row_sums[4],
        clipped,
        factors,
    )


def solution(mesh):
    in_specs = (
        P(("dp", "expert"), None),
        P("dp", "expert"),
        P("dp", "expert"),
        P("dp", "expert"),
        P(None, "expert"),
        P("expert", None, "dp"),
        P("expert", "dp", None),
        P(("dp", "expert"), None),
        P(),
        P(("dp", "expert"), None),
    )
    out_specs = (
        P(("dp", "expert"), None),
        P(("dp", "expert"), None),
        P("dp", "expert"),
        P("dp", "expert"),
        P("dp", "expert"),
        P(None, "expert"),
        P("expert", None, "dp"),
        P("expert", "dp", None),
        P("dp", "expert"),
        P(),
    )
    fits = mesh.shape["dp"] == 4 and mesh.shape["expert"] == 8
    return jax.shard_map(fused if fits else shards, mesh=mesh, in_specs=in_specs, out_specs=out_specs, check_vma=False)
```

```python
import functools

import jax
import jax.numpy as jnp
from jax import lax
from jax.experimental import pallas as pl
from jax.experimental.pallas import tpu as pltpu
from jax.sharding import PartitionSpec as P

D = 512
HEADS = 8
HEAD = 64
SEQ = 197
EPS = 1e-06
LEARN = 0.001
SEQP = 208
BF = jnp.bfloat16
F32 = jnp.float32
MESH = pl.DeviceIdType.MESH
ORDER = (0, 1, 2, 3)

(DENSE_Z, DENSE_X, DENSE_Y, DENSE_C, EXPW, CROSS, COT, ACT, GATE, DXE, ZED, DGATE, WGC, WGY, RSC, RSD, RSY, RSX, RSZ, SMC,
 SME) = range(21)


def dg(left, right, left_dim, right_dim):
    return lax.dot_general(
        left, right, (((left_dim,), (right_dim,)), ((), ())), preferred_element_type=F32
    )


def iota(shape, dim):
    return lax.broadcasted_iota(jnp.int32, shape, dim)


def eye(size, dtype=BF):
    return (iota((size, size), 0) == iota((size, size), 1)).astype(F32).astype(dtype)


def split_two(value):
    high = value.astype(BF)
    return high, (value - high.astype(F32)).astype(BF)


def to_row(column):
    size = column.shape[0]
    return jnp.sum(jnp.where(iota((size, size), 0) == iota((size, size), 1), column, 0.0), axis=0, keepdims=True)


def to_column(row):
    size = row.shape[1]
    return jnp.sum(jnp.where(iota((size, size), 0) == iota((size, size), 1), row, 0.0), axis=1, keepdims=True)


def norm_parts(values):
    centered = values - jnp.mean(values, axis=-1, keepdims=True)
    inverse = lax.rsqrt(jnp.mean(centered * centered, axis=-1, keepdims=True) + EPS)
    return centered * inverse, inverse


def norm_back(upstream, normed, inverse, gain):
    scaled = upstream * gain
    inner = scaled - jnp.mean(scaled, axis=-1, keepdims=True)
    inner = inner - normed * jnp.mean(scaled * normed, axis=-1, keepdims=True)
    return (
        inverse * inner,
        jnp.sum(upstream * normed, axis=0, keepdims=True),
        jnp.sum(upstream, axis=0, keepdims=True),
    )


def normal_parts(u):
    return 0.5 + 0.5 * lax.erf(u * 2.0 ** -0.5), u * (jnp.exp(-0.5 * u * u) * 0.3989422804014327)


def block_kernel(
    n_e, cap, rows,
    tok_in, cot_in, routes_in, w_qkv, w_out, w_router_in, norm_in, win, wdown, threshold,
    *refs,
):
    outs_hbm, staged, refs = refs[:10], refs[10:20], refs[20:]
    block_out, grad_tok, grad_qkv, grad_out, grad_router, grad_norm, grad_in, grad_down, clipped, factors = staged
    (
        tok, cot, routes, w_router, norm,
        GB, WI, WD, XF, CP, R, A1, A2, QKV, O, PS, SEL, SELT, SLOT, NRM, PR, WR,
        SA, SB, CR, AR, ZR, DXR, GS, GR, GCOL, DGS, DGR, H, DU, DZ,
        WCS, WCR, WYR, DQKV, DR, GG, RCR, RDS, RDR, RYS, RYR, RXS, RXR, RZS, RZR, SM, SMCR, SMER,
        SLT, SLF, XC, XA, XDR, XZR,
        send, recv, local, leave,
    ) = refs
    dp = lax.axis_index("dp")
    me = lax.axis_index("expert")
    core = lax.rem(dp, 2)
    dp_c = dp + 1 - 2 * core
    dp_y = lax.rem(dp + 2, 4)
    dp_cy = lax.rem(dp_c + 2, 4)
    images = rows // SEQ
    T = images * SEQP
    part = 3 * D // n_e
    opart = D // n_e
    bundle = part + opart + 16

    half_n = n_e // 2
    group, place = lax.div(me, half_n), lax.rem(me, half_n)
    mirror = lax.rem(me + half_n, n_e)
    zz, xx = lax.div(me, 2), lax.rem(me, 2)
    z_n = n_e // 2

    def at_off(i):
        return lax.rem(me + i, n_e)

    def to_of(s):
        return lax.rem(group + s // half_n, 2) * half_n + lax.rem(place + s % half_n, half_n)

    def from_of(s):
        return lax.rem(group + s // half_n, 2) * half_n + lax.rem(place + half_n - s % half_n, half_n)

    def near(i):
        return group * half_n + lax.rem(place + i, half_n)

    def near_from(i):
        return group * half_n + lax.rem(place + half_n - i % half_n, half_n)

    def column(dz, other=0):
        return lax.rem(zz + z_n + dz, z_n) * 2 + lax.rem(xx + other, 2)

    pending = {}

    def remote(src, dst, kind, i, where):
        return pltpu.make_async_remote_copy(
            src_ref=src, dst_ref=dst, send_sem=send.at[kind, i], recv_sem=recv.at[kind, i],
            device_id=where, device_id_type=MESH,
        )

    def begin(kind, i, copy):
        pending[kind, i] = copy
        copy.start()

    def sent(kind, i):
        pending.pop((kind, i)).wait_send()

    def brow(e, start=0, size=None):
        return pl.ds(pl.multiple_of(bundle * e + start, 16), bundle if size is None else size)

    peers = [(dp, at_off(i)) for i in range(1, n_e)] + [(dp_y, me), (dp_c, me)]
    barrier = pltpu.get_barrier_semaphore()
    for p in peers:
        pl.semaphore_signal(barrier, inc=1, device_id=p, device_id_type=MESH)
    load_in = pltpu.make_async_copy(win, WI.at[dp], local.at[0])
    load_down = pltpu.make_async_copy(wdown, WD.at[dp], local.at[1])
    loads = [
        pltpu.make_async_copy(src, dst, local.at[2 + k])
        for k, (src, dst) in enumerate((
            (w_qkv, GB.at[dp, brow(me, 0, part)]), (w_out, GB.at[dp, brow(me, part, opart)]), (w_router_in, w_router),
            (norm_in, norm), (cot_in, cot), (tok_in, tok), (routes_in, routes),
        ))
    ]
    for load in loads:
        load.start()
    load_in.start()
    load_down.start()
    for load in loads:
        load.wait()

    def deliver_now(k):
        copy = pltpu.make_async_copy(staged[k], outs_hbm[k], leave.at[k])
        copy.start()
        leaving.append(copy)

    leaving = []

    spread = (iota((16, 4), 0) == iota((16, 4), 1)).astype(F32).astype(BF)
    twice = (lax.rem(iota((HEAD, 128), 1), HEAD) == iota((HEAD, 128), 0)).astype(F32).astype(BF)
    small = dg(dg(spread, norm[...], 1, 0).astype(BF), twice, 1, 0)
    small = jnp.where(iota((16, 128), 0) == 8, w_router[...].astype(F32), small)
    GB[dp, brow(me, part + opart, 16), :] = small.astype(BF)

    move = ((lax.div(iota((T, rows), 0), SEQP) * SEQ + lax.rem(iota((T, rows), 0), SEQP) == iota((T, rows), 1))
            & (lax.rem(iota((T, rows), 0), SEQP) < SEQ)).astype(F32).astype(BF)
    CP[...] = dg(move, cot[...], 1, 0).astype(BF)
    XF[...] = dg(move, tok[...], 1, 0)
    pl.semaphore_wait(barrier, len(peers))

    def dense(kind, i, d, e, where):
        return remote(GB.at[d, brow(e)], GB.at[d, brow(e)], kind, i, where)

    def dense_z(dz, e):
        return dense(DENSE_Z, dz, dp, e, (dp, column(dz)))

    def dense_x(dz, e, d=dp):
        return dense(DENSE_X, dz, d, e, (dp, column(0, 1)))

    def dense_y(dz, e):
        return dense(DENSE_Y, dz, dp, e, (dp_y, me))

    def dense_c(i):
        d = dp if i == 0 else dp_y
        return remote(GB.at[d], GB.at[d], DENSE_C, i, (dp_c, me))

    for dz in (2, 1, 3):
        begin(DENSE_Z, dz, dense_z(dz, me))
    begin(DENSE_X, 0, dense_x(0, me))
    begin(DENSE_Y, 0, dense_y(0, me))

    which = routes[...]
    block = lax.rem(lax.rem(which, half_n) + half_n - place, half_n)
    away = jnp.where(lax.div(which, half_n) == group, block, block + half_n)
    named = (away[0:1] == iota((n_e, rows), 0)) | (away[1:2] == iota((n_e, rows), 0))
    named = named.astype(F32).astype(BF)
    chosen = dg(move, named, 1, 1)
    before = (iota((T, T), 1) < iota((T, T), 0)).astype(F32).astype(BF)
    chosen_low = chosen.astype(BF)
    slot = jnp.where(chosen > 0.5, dg(before, chosen_low, 1, 0), -1.0)
    SLOT[...] = slot
    chosen_t = dg(named, move, 1, 1)
    slot_t = jnp.where(chosen_t > 0.5, dg(chosen_t.astype(BF), before, 1, 1), -1.0)
    SLT[...] = slot_t
    slots_over = remote(SLT, SLF, CROSS, 0, (dp, mirror))
    cot_over = remote(CP, XC, CROSS, 1, (dp, mirror))
    lane = iota((T, 2 * cap), 1).astype(F32)
    level = iota((cap, T), 0).astype(F32)

    def choose(first, columns, rows_of):
        for k in range(half_n // 2):
            target = jnp.where(lane < cap, columns[:, 2 * k:2 * k + 1], columns[:, 2 * k + 1:2 * k + 2] + cap)
            at = cap * (first + 2 * k)
            SELT[:, at:at + 2 * cap] = (lane == target).astype(F32).astype(BF)
        for i in range(half_n):
            SEL[first + i] = (level == rows_of[i:i + 1, :]).astype(F32).astype(BF)

    choose(0, slot, slot_t)

    def pack(source, first, buf_s, buf_r, kind):
        for i in (2, 1, 3, 0):
            s = first + i
            packed = dg(SEL[s], source[...], 1, 0).astype(BF)
            if i == 0:
                buf_r[cap * s:cap * (s + 1)] = packed
            else:
                buf_s[cap * s:cap * (s + 1)] = packed
                begin(kind, s, near_copy(buf_s, buf_r, kind, s, near(i)))

    def near_copy(buf_s, buf_r, kind, s, e):
        return remote(buf_s.at[pl.ds(cap * s, cap)], buf_r.at[pl.ds(cap * s, cap)], kind, s, (dp, e))

    for dz in range(1, z_n):
        dense_z(dz, column(-dz)).wait_recv()
        begin(DENSE_X, dz, dense_x(dz, column(-dz)))
        begin(DENSE_Y, dz, dense_y(dz, column(-dz)))
    begin(CROSS, 0, slots_over)
    begin(CROSS, 1, cot_over)
    pack(CP, 0, SA, CR, COT)
    for dz in range(z_n):
        dense_x(dz, column(-dz, 1)).wait_recv()
        if dz < z_n // 2:
            begin(DENSE_Y, z_n + dz, dense_y(z_n + dz, column(-dz, 1)))
        dense_y(dz, column(-dz)).wait_recv()
        if dz >= z_n // 2:
            begin(DENSE_X, z_n + dz, dense_x(z_n + dz, column(-dz), dp_y))
    begin(DENSE_C, 0, dense_c(0))

    load_in.wait()
    load_down.wait()

    def exp_w(k):
        buf = WI if k % 2 == 0 else WD
        if k < 2:
            return remote(buf.at[dp], buf.at[dp], EXPW, k, (dp_y, me))
        d = dp if k < 4 else dp_y
        return remote(buf.at[d], buf.at[d], EXPW, k, (dp_c, me))

    for k in range(4):
        begin(EXPW, k, exp_w(k))

    half = iota((16, 128), 1) < HEAD
    pieces = []
    for k in range(D // 128):
        even = GB[dp, brow(2 * k, part + opart, 16), :].astype(F32)
        odd = GB[dp, brow(2 * k + 1, part + opart, 16), :].astype(F32)
        pieces.append(jnp.where(half, even, odd))
    NRM[...] = jnp.concatenate(pieces, axis=1)
    normed, _ = norm_parts(XF[...])
    A1[...] = (normed * NRM[0:1] + NRM[1:2]).astype(BF)

    for dz in range(z_n):
        if dz < z_n // 2:
            dense_y(z_n + dz, column(-dz, 1)).wait_recv()
        else:
            dense_x(z_n + dz, column(-dz, 1), dp_y).wait_recv()
    begin(DENSE_C, 1, dense_c(1))
    dense_c(0).wait_recv()
    dense_c(1).wait_recv()

    def dense_rows(e, start, size):
        return jnp.concatenate([GB[d, brow(e, start, size), :] for d in range(4)], axis=1)

    def qkv_weight(k):
        return jnp.concatenate([dense_rows(2 * k, 0, part), dense_rows(2 * k + 1, 0, part)], axis=0)

    def out_weight():
        return jnp.concatenate([dense_rows(e, part, opart) for e in range(n_e)], axis=0)

    for k in range(n_e // 2):
        QKV[:, 2 * part * k:2 * part * (k + 1)] = dg(A1[...], qkv_weight(k), 1, 1).astype(BF)

    row_ok = iota((SEQP, SEQP), 0) < SEQ
    col_ok = iota((SEQP, SEQP), 1) < SEQ
    first_head = iota((1, 128), 1) < HEAD
    masks = [first_head.astype(F32).astype(BF), (~first_head).astype(F32).astype(BF)]

    def attend(g, peaks):
        img = lax.div(g, HEADS // 2)
        pair = lax.rem(g, HEADS // 2)
        at = pl.ds(pl.multiple_of(SEQP * img, 16), SEQP)
        q2 = QKV[at, pl.ds(pl.multiple_of(128 * pair, 128), 128)]
        k2 = QKV[at, pl.ds(pl.multiple_of(D + 128 * pair, 128), 128)]
        v2 = QKV[at, pl.ds(pl.multiple_of(2 * D + 128 * pair, 128), 128)]
        mixed = jnp.zeros((SEQP, 128), F32)
        for hh in range(2):
            s = dg(q2 * masks[hh], k2, 1, 1) * HEAD ** -0.5
            s = jnp.where(col_ok, s, -1e30)
            top = jnp.max(s, axis=1, keepdims=True)
            ex = jnp.exp(s - top)
            p = ex / jnp.sum(ex, axis=1, keepdims=True)
            PS[2 * g + hh] = p
            mixed = mixed + dg(p.astype(BF), v2 * masks[hh], 1, 0)
            peak = jnp.max(jnp.where(row_ok, s, -1e30), axis=(0, 1), keepdims=True)
            peaks = jnp.where(iota((8, 128), 0) == 2 * pair + hh, jnp.maximum(peaks, peak), peaks)
        O[at, pl.ds(pl.multiple_of(128 * pair, 128), 128)] = mixed.astype(BF)
        return peaks

    peaks = lax.fori_loop(0, images * HEADS // 2, attend, jnp.full((8, 128), -1e30, F32), unroll=True)
    for k in range(D // 128):
        SM[0, k, 8:16, :] = peaks

    R[...] = XF[...] + dg(O[...], out_weight(), 1, 1)
    normed, _ = norm_parts(R[...])
    A2[...] = (normed * NRM[2:3] + NRM[3:4]).astype(BF)
    act_over = remote(A2, XA, CROSS, 2, (dp, mirror))
    begin(CROSS, 2, act_over)
    pack(A2, 0, SB, AR, ACT)
    router = jnp.zeros((n_e, D), F32)
    for i in range(n_e):
        at = dense_rows(to_of(i), part + opart, 16).astype(F32)
        router = jnp.where(iota((n_e, D), 0) == i, at[8:9, :], router)
    WR[...] = router.astype(BF)
    logits = dg(A2[...], WR[...], 1, 1)
    ex = jnp.exp(logits - jnp.max(logits, axis=1, keepdims=True))
    PR[...] = ex / jnp.sum(ex, axis=1, keepdims=True)
    lane_cap = iota((T, cap), 1).astype(F32)

    def gate_copy(i):
        return remote(GS.at[i], GR.at[i], GATE, i, (dp, to_of(i)))

    for i in range(n_e):
        gate = SLOT[:, i:i + 1]
        gate = jnp.sum(jnp.where(lane_cap == gate, PR[:, i:i + 1], 0.0), axis=0, keepdims=True)
        if i == 0:
            GR[0] = jnp.broadcast_to(gate, (8, cap))
        else:
            GS[i] = jnp.broadcast_to(gate, (8, cap))
            begin(GATE, i, gate_copy(i))

    for k in range(2):
        exp_w(k).wait_recv()
        begin(EXPW, 4 + k, exp_w(4 + k))
    for k in range(2, 6):
        exp_w(k).wait_recv()

    slots_over.wait_recv()
    cot_over.wait_recv()
    slot_f = SLF[...]
    choose(half_n, dg(eye(T), slot_f[half_n:].astype(BF), 1, 1), slot_f[half_n:])
    pack(XC, half_n, SA, CR, COT)

    pairs = n_e // 2

    def dgate_copy(i):
        return remote(DGS.at[i], DGR.at[i], DGATE, i, (dp, from_of(i)))

    act_over.wait_recv()
    pack(XA, half_n, SB, AR, ACT)
    for j in ORDER:
        mine = pl.ds(2 * cap * j, 2 * cap)
        gates = []
        for i in (2 * j, 2 * j + 1):
            if i % half_n:
                near_copy(SA, CR, COT, i, near(i)).wait_recv()
                near_copy(SB, AR, ACT, i, near(i)).wait_recv()
                sent(COT, i)
                sent(ACT, i)
            if i > 0:
                gate_copy(i).wait_recv()
            gates.append(to_column(GR[i, 0:1, :]))
        gate = jnp.concatenate(gates, axis=0)
        GCOL[...] = gate
        DZ[mine] = (CR[mine].astype(F32) * gate).astype(BF)

        for q in range(8):
            d, at, to = q // 2, slice(256 * (q % 2), 256 * (q % 2) + 256), slice(256 * q, 256 * q + 256)
            u = dg(AR[mine], WI[d, :, at], 1, 0)
            dh = dg(CR[mine], WD[d, at, :], 1, 1)
            phi, slope = normal_parts(u)
            H[mine, to] = (u * phi).astype(BF)
            DU[mine, to] = (dh * (phi + slope) * GCOL[...]).astype(BF)
        z = dg(H[mine, :], WD[...].reshape(4 * 512, D), 1, 0)
        dx = dg(DU[mine, :], jnp.concatenate([WI[d] for d in range(4)], axis=1), 1, 1)
        z_low = z.astype(BF).astype(F32)
        dgate = jnp.sum(CR[mine].astype(F32) * z_low, axis=1, keepdims=True)
        z_out = (z_low * gate).astype(BF)
        dx_out = dx.astype(BF)
        for b, i in enumerate((2 * j, 2 * j + 1)):
            row = jnp.broadcast_to(to_row(dgate[cap * b:cap * (b + 1)]), (8, cap))
            at = slice(cap * i, cap * (i + 1))
            if i % half_n == 0:
                DXR[at] = dx_out[cap * b:cap * (b + 1)]
                ZR[at] = z_out[cap * b:cap * (b + 1)]
            else:
                SB[at] = dx_out[cap * b:cap * (b + 1)]
                SA[at] = z_out[cap * b:cap * (b + 1)]
                begin(DXE, i, near_copy(SB, DXR, DXE, i, near_from(i)))
            if i == 0:
                DGR[0] = row
            else:
                DGS[i] = row
                begin(DGATE, i, dgate_copy(i))

    mine = slice(0, cap * half_n)
    theirs = slice(cap * half_n, cap * n_e)

    def give_back(buf_r, kind, k, buf_s, over):
        for i in range(1, half_n):
            near_copy(SA, buf_r, kind, half_n + i, near_from(i)).wait_recv()
        buf_s[...] = dg(SELT[:, theirs], buf_r[theirs], 1, 0).astype(BF)
        begin(CROSS, k, over)

    sent_over = remote(XC, XDR, CROSS, 3, (dp, mirror))
    z_over = remote(XA, XZR, CROSS, 4, (dp, mirror))
    give_back(DXR, DXE, 3, XC, sent_over)
    def wg(d, w, store):
        cols = pl.ds(pl.multiple_of(512 * d, 512), 512)

        def half_of(m, carry):
            to = pl.ds(pl.multiple_of(256 * m, 256), 256)
            if w == 0:
                store(to, dg(AR[:, to], DU[:, cols], 0, 0))
            else:
                store(to, dg(H[:, pl.ds(pl.multiple_of(512 * d + 256 * m, 256), 256)], DZ[...], 0, 0))
            return carry

        lax.fori_loop(0, 2, half_of, 0)

    yy = lax.div(dp, 2)
    def wgc(jy, w):
        return remote(WCS.at[2 * jy + w], WCR.at[2 * jy + w], WGC, 2 * jy + w, (dp_c, me))

    def wgy(w):
        return remote(WCS.at[2 + w], WYR.at[w], WGY, w, (dp_y, me))

    for jy in (1, 0):
        for w in range(2):
            def store(to, value, at=2 * jy + w):
                WCS[at, to, :] = value.astype(BF)

            wg(lax.rem(yy + jy, 2) * 2 + 1 - core, w, store)
            begin(WGC, 2 * jy + w, wgc(jy, w))
    for i in (5, 6, 7, 1, 2, 3):
        begin(ZED, i, near_copy(SA, ZR, ZED, i, near_from(i)))
    for w in range(2):
        wgc(1, w).wait_recv()
        sent(WGC, 2 + w)

        def store(to, value, at=2 + w):
            WCS[at, to, :] = (value + WCR[at, to, :].astype(F32)).astype(BF)

        wg(dp_y, w, store)
        begin(WGY, w, wgy(w))
    for w, out in enumerate((grad_in, grad_down)):
        wgc(0, w).wait_recv()

        def store(to, value, out=out, at=w):
            out[to, :] = value + WCR[at, to, :].astype(F32)

        wg(dp, w, store)

    for i in range(1, n_e):
        dgate_copy(i).wait_recv()
        if i < half_n:
            near_copy(SB, DXR, DXE, i, near_from(i)).wait_recv()
    sent_over.wait_recv()
    lane_e = iota((T, n_e), 1)
    dprob = jnp.zeros((T, n_e), F32)
    for i in range(n_e):
        got = jnp.sum(jnp.where(lane_cap == SLOT[:, i:i + 1], DGR[i, 0:1, :], 0.0), axis=1, keepdims=True)
        dprob = jnp.where(lane_e == i, got, dprob)
    prob = PR[...]
    dlogit = prob * (dprob - jnp.sum(dprob * prob, axis=1, keepdims=True))
    high, low = split_two(dlogit)
    da2 = dg(SELT[:, mine], DXR[mine], 1, 0) + XDR[...].astype(F32)
    da2 = da2 + dg(high, WR[...], 1, 0) + dg(low, WR[...], 1, 0)
    g_router = dg(high, A2[...], 0, 0) + dg(low, A2[...], 0, 0)
    normed, inverse = norm_parts(R[...])
    back, g_gain2, g_shift2 = norm_back(da2, normed, inverse, NRM[2:3])
    DR[...] = CP[...].astype(F32) + back
    dy = DR[...].astype(BF)
    sent(CROSS, 1)
    DO = CP
    DO[...] = dg(dy, out_weight(), 1, 0).astype(BF)
    g_out = dg(dy, O[...], 0, 0).astype(BF)

    def attend_back(g, carry):
        img = lax.div(g, HEADS // 2)
        pair = lax.rem(g, HEADS // 2)
        at = pl.ds(pl.multiple_of(SEQP * img, 16), SEQP)
        cq = pl.ds(pl.multiple_of(128 * pair, 128), 128)
        ck = pl.ds(pl.multiple_of(D + 128 * pair, 128), 128)
        cv = pl.ds(pl.multiple_of(2 * D + 128 * pair, 128), 128)
        q2, k2, v2, do2 = QKV[at, cq], QKV[at, ck], QKV[at, cv], DO[at, cq]
        dq = dk = dv = jnp.zeros((SEQP, 128), F32)
        for hh in range(2):
            p = PS[2 * g + hh]
            do_h = do2 * masks[hh]
            dpr = dg(do_h, v2, 1, 1)
            ds = (p * (dpr - jnp.sum(dpr * p, axis=1, keepdims=True))).astype(BF)
            dq = dq + dg(ds, k2 * masks[hh], 1, 0)
            dk = dk + dg(ds, q2 * masks[hh], 0, 0)
            dv = dv + dg(p.astype(BF), do_h, 0, 0)
        DQKV[at, cq] = (dq * HEAD ** -0.5).astype(BF)
        DQKV[at, ck] = (dk * HEAD ** -0.5).astype(BF)
        DQKV[at, cv] = dv.astype(BF)
        return carry

    lax.fori_loop(0, images * HEADS // 2, attend_back, 0)

    give_back(ZR, ZED, 4, XA, z_over)

    for k in range(n_e // 2):
        g2 = dg(DQKV[:, 2 * part * k:2 * part * (k + 1)], A1[...], 0, 0).astype(BF)
        for b in range(2):
            e = 2 * k + b
            ro = jnp.zeros((1, D), F32)
            for i in range(n_e):
                ro = jnp.where(to_of(i) == e, g_router[i:i + 1, :], ro)
            foot = jnp.where(iota((16, D), 0) == 8, ro, 0.0).astype(BF)
            for d in range(4):
                cols = slice(128 * d, 128 * (d + 1))
                GG[d, brow(e, 0, part), :] = g2[part * b:part * (b + 1), cols]
                GG[d, brow(e, part, opart), :] = g_out[opart * e:opart * (e + 1), cols]
                GG[d, brow(e, part + opart, 16), :] = foot[:, cols]

    def rsc(k):
        d = dp_c if k == 0 else dp_cy
        return remote(GG.at[d], RCR.at[k], RSC, k, (dp_c, me))

    begin(RSC, 1, rsc(1))
    begin(RSC, 0, rsc(0))

    da1 = jnp.zeros((T, D), F32)
    for k in range(n_e // 2):
        da1 = da1 + dg(DQKV[:, 2 * part * k:2 * part * (k + 1)], qkv_weight(k), 1, 0)
    normed, inverse = norm_parts(XF[...])
    back, g_gain1, g_shift1 = norm_back(da1, normed, inverse, NRM[0:1])
    gtok = (DR[...] + back).astype(BF)
    grad_tok[...] = dg(move, gtok, 0, 0).astype(BF)
    deliver_now(1)
    row8 = iota((8, D), 0)
    stack = jnp.where(row8 == 0, g_gain1, jnp.where(row8 == 1, g_shift1, jnp.where(row8 == 2, g_gain2, jnp.where(row8 == 3, g_shift2, 0.0))))
    for k in range(D // 128):
        SM[0, k, 0:8, :] = stack[:, 128 * k:128 * (k + 1)]

    def smc(k):
        return remote(SM.at[k], SMCR.at[k], SMC, k, (dp_c if k == 0 else dp_y, me))

    def sm_join(a, b):
        is_sum = iota(a.shape, len(a.shape) - 2) < 8
        return jnp.where(is_sum, a + b, jnp.maximum(a, b))

    begin(SMC, 0, smc(0))
    smc(0).wait_recv()
    SM[1] = sm_join(SM[0], SMCR[0])
    begin(SMC, 1, smc(1))

    def rs_send(buf_s, buf_r, kind, i, where):
        return remote(buf_s.at[i], buf_r.at[i], kind, i, where)

    x_peer, y_peer = (dp, column(0, 1)), (dp_y, me)
    mid = z_n // 2

    def rsd(dz):
        return rs_send(RDS, RDR, RSD, dz, y_peer if dz < mid else x_peer)

    def rsx(dz):
        return rs_send(RXS, RXR, RSX, dz, x_peer)

    def rsy(dz):
        return rs_send(RYS, RYR, RSY, dz, y_peer)

    def rsz(dz):
        return rs_send(RZS, RZR, RSZ, dz, (dp, column(dz)))

    def core_sum(k, dz, other):
        at = brow(column(dz, other))
        return GG[dp_y if k else dp, at, :].astype(F32) + RCR[k, at, :].astype(F32)

    rsc(1).wait_recv()
    for dz in (1, 3, 0, 2):
        RDS[dz] = core_sum(1, dz, 1).astype(BF)
        begin(RSD, dz, rsd(dz))
    rsc(0).wait_recv()
    for dz in (1, 0, 3, 2):
        x_sum, y_sum = core_sum(0, dz, 1), core_sum(1, dz, 0)
        if dz < mid:
            RYS[dz] = y_sum.astype(BF)
            begin(RSY, dz, rsy(dz))
        else:
            RXS[dz] = x_sum.astype(BF)
            begin(RSX, dz, rsx(dz))
    for dz in (1, 3, 2, 0):
        rsd(dz).wait_recv()
        if dz < mid:
            RXS[dz] = (core_sum(0, dz, 1) + RDR[dz].astype(F32)).astype(BF)
            begin(RSX, dz, rsx(dz))
        else:
            RYS[dz] = (core_sum(1, dz, 0) + RDR[dz].astype(F32)).astype(BF)
            begin(RSY, dz, rsy(dz))
    dense_sum = None
    for dz in (1, 3, 2, 0):
        rsx(dz).wait_recv()
        rsy(dz).wait_recv()
        total = core_sum(0, dz, 0) + RXR[dz].astype(F32) + RYR[dz].astype(F32)
        if dz:
            RZS[dz] = total.astype(BF)
            begin(RSZ, dz, rsz(dz))
        else:
            dense_sum = total
    smc(1).wait_recv()
    SM[2] = sm_join(SM[1], SMCR[1])

    def sme(i):
        return remote(SM.at[2, lax.div(at_off(i), 2)], SMER.at[i], SME, i, (dp, at_off(i)))

    for i in range(1, n_e):
        begin(SME, i, sme(i))
    for dz in range(1, z_n):
        rsz(dz).wait_recv()
        dense_sum = dense_sum + RZR[dz].astype(F32)
    tiny = SM[2, lax.div(me, 2)]
    for i in range(1, n_e):
        sme(i).wait_recv()
        tiny = sm_join(tiny, SMER[i])

    g_qkv = dense_sum[0:part]
    grad_qkv[...] = g_qkv
    grad_out[...] = dense_sum[part:part + opart]
    grad_router[...] = dense_sum[part + opart + 8:part + opart + 9]
    grad_norm[...] = jnp.where(lax.rem(me, 2) == 0, tiny[0:4, 0:HEAD], tiny[0:4, HEAD:128])
    scale = jnp.sqrt(jnp.minimum(1.0, threshold[0].astype(F32) / tiny[8:16, :]))
    diagonal = jnp.where(iota((8, 128), 0) == iota((8, 128), 1), scale, 0.0)
    factors[...] = jnp.sum(diagonal, axis=0, keepdims=True)[:, 0:HEADS]
    column = me * part + iota((part, 128), 0)
    head = jnp.where(column < 2 * D, lax.rem(lax.div(column, HEAD), HEADS), HEADS)
    by_column = jnp.ones((part, 128), F32)
    for h in range(HEADS):
        by_column = jnp.where(head == h, scale[h:h + 1, :], by_column)
    clipped[...] = (GB[dp, brow(me, 0, part), :].astype(F32) - LEARN * g_qkv) * by_column
    for k in (2, 3, 4, 5, 8, 9):
        deliver_now(k)

    for w, out in enumerate((grad_in, grad_down)):
        wgy(w).wait_recv()
        out[...] = out[...] + WYR[w].astype(F32)
        deliver_now(6 + w)

    for i in range(1, half_n):
        near_copy(SA, ZR, ZED, i, near_from(i)).wait_recv()
    z_over.wait_recv()
    total = R[...] + dg(SELT[:, mine], ZR[mine], 1, 0) + XZR[...].astype(F32)
    block_out[...] = dg(move, total.astype(BF), 0, 0).astype(BF)
    deliver_now(0)

    for copy in leaving:
        copy.wait()
    for kind, i in list(pending):
        sent(kind, i)


def deliver(*refs):
    spots = len(refs) // 2
    done = refs[-1]
    copies = [pltpu.make_async_copy(refs[i], refs[spots + i], done.at[i]) for i in range(spots)]
    for copy in copies:
        copy.start()
    for copy in copies:
        copy.wait()


def fused(tokens, w_qkv, w_out, w_router, norm_params, w_in, w_down, routes, threshold, cotangent):
    rows = tokens.shape[0]
    n_e = lax.axis_size("expert")
    images = rows // SEQ
    T = images * SEQP
    cap = 15 * routes.shape[1] * rows // (8 * n_e)
    cap = -(-cap // 16) * 16
    slots = n_e * cap
    part, opart = w_qkv.shape[1], w_out.shape[1]
    drows = w_qkv.shape[0]
    bundle = part + opart + 16
    ff = w_in.shape[2]
    V = pltpu.VMEM
    spec = pl.BlockSpec(memory_space=pltpu.VMEM)
    any_spec = pl.BlockSpec(memory_space=pl.ANY)
    S = jax.ShapeDtypeStruct
    results = (
        S((rows, D), BF), S((rows, D), BF), S((part, drows), F32), S((opart, drows), F32), S((1, drows), F32),
        S((4, HEAD), F32), S((D, ff), F32), S((ff, D), F32), S((part, drows), F32), S((1, HEADS), F32),
    )
    outs = pl.pallas_call(
        functools.partial(block_kernel, n_e, cap, rows),
        out_shape=results,
        in_specs=[any_spec] * 9 + [pl.BlockSpec(memory_space=pltpu.SMEM)],
        out_specs=[any_spec] * 10,
        scratch_shapes=[V(o.shape, o.dtype) for o in results] + [
            V((rows, D), BF), V((rows, D), BF), V((2, rows), jnp.int32), V((1, drows), BF), V((4, HEAD), BF),
            V((4, n_e * bundle, 128), BF), V((4, D, ff), BF), V((4, ff, D), BF), V((T, D), F32), V((T, D), BF),
            V((T, D), F32), V((T, D), BF), V((T, D), BF), V((T, 3 * D), BF), V((T, D), BF),
            V((images * HEADS, SEQP, SEQP), F32), V((n_e, cap, T), BF), V((T, slots), BF), V((T, n_e), F32),
            V((16, D), F32), V((T, n_e), F32), V((n_e, D), BF),
            V((slots, D), BF), V((slots, D), BF), V((slots, D), BF), V((slots, D), BF), V((slots, D), BF), V((slots, D), BF),
            V((n_e, 8, cap), F32), V((n_e, 8, cap), F32), V((2 * cap, 1), F32), V((n_e, 8, cap), F32), V((n_e, 8, cap), F32),
            V((slots, 4 * ff), BF), V((slots, 4 * ff), BF), V((slots, D), BF),
            V((4, D, ff), BF), V((4, D, ff), BF), V((2, D, ff), BF),
            V((T, 3 * D), BF), V((T, D), F32),
            V((4, n_e * bundle, 128), BF), V((2, n_e * bundle, 128), BF),
            *[V((n_e // 2, bundle, 128), BF)] * 8,
            V((3, D // 128, 16, 128), F32), V((2, D // 128, 16, 128), F32), V((n_e, 16, 128), F32),
            V((n_e, T), F32), V((n_e, T), F32), V((T, D), BF), V((T, D), BF), V((T, D), BF), V((T, D), BF),
            pltpu.SemaphoreType.DMA((21, 8)), pltpu.SemaphoreType.DMA((21, 8)), pltpu.SemaphoreType.DMA((9,)),
            pltpu.SemaphoreType.DMA((10,)),
        ],
        compiler_params=pltpu.CompilerParams(
            collective_id=0, has_side_effects=True, vmem_limit_bytes=63 * 2 ** 20
        ),
    )(
        tokens, cotangent, routes.T, w_qkv.T, w_out.T, w_router.T, norm_params,
        w_in.reshape(D, ff), w_down.reshape(ff, D), threshold,
    )
    spots = len(outs)
    outs = pl.pallas_call(
        deliver,
        out_shape=tuple(S(o.shape, o.dtype) for o in outs),
        in_specs=[spec] * spots,
        out_specs=[any_spec] * spots,
        scratch_shapes=[pltpu.SemaphoreType.DMA((spots,))],
    )(*outs)
    block_out, grad_tok, grad_qkv, grad_out, grad_router, grad_norm, grad_in, grad_down, clipped, factors = outs
    return (
        block_out, grad_tok, grad_qkv.T, grad_out.T, grad_router.T, grad_norm,
        grad_in[None], grad_down[None], clipped.T, factors.reshape(HEADS),
    )


def layer_norm(values, norm_gain, norm_shift):
    center = jnp.mean(values, axis=-1, keepdims=True)
    centered = values - center
    inverse = lax.rsqrt(jnp.mean(centered * centered, axis=-1, keepdims=True) + EPS)
    normed = centered * inverse
    return (normed * norm_gain + norm_shift, normed, inverse)


def plain_norm_back(upstream, normed, inverse, norm_gain):
    scaled = upstream * norm_gain
    inner_term = (
        scaled
        - jnp.mean(scaled, axis=-1, keepdims=True)
        - normed * jnp.mean(scaled * normed, axis=-1, keepdims=True)
    )
    return (inverse * inner_term, jnp.sum(upstream * normed, axis=0), jnp.sum(upstream, axis=0))


def exact_gelu(inputs):
    return jax.nn.gelu(inputs, approximate=False)


def scores_of(queries, key_part):
    return jnp.einsum(
        "bqhd,bkhd->bhqk", queries, key_part, preferred_element_type=jnp.float32
    ) * HEAD ** (-0.5)


def contract_rows(left, right):
    return lax.dot_general(
        left, right, (((0,), (0,)), ((), ())), preferred_element_type=jnp.float32
    )


def contract_cols(left, right):
    return lax.dot_general(
        left, right, (((1,), (1,)), ((), ())), preferred_element_type=jnp.float32
    )


def fetch_forward(w_qkv, w_out, w_router, norm_params, w_in, w_down):
    col_parts = (
        lax.all_gather(w_qkv, "expert", axis=1, tiled=True),
        lax.all_gather(w_out, "expert", axis=1, tiled=True),
        lax.all_gather(w_router, "expert", axis=1, tiled=True),
        lax.all_gather(norm_params, "expert", axis=1, tiled=True),
    )
    full_parts = (
        lax.all_gather(col_parts[0], "dp", axis=0, tiled=True),
        lax.all_gather(col_parts[1], "dp", axis=0, tiled=True),
        lax.all_gather(col_parts[2], "dp", axis=0, tiled=True),
        lax.all_gather(w_in, "dp", axis=2, tiled=True),
        lax.all_gather(w_down, "dp", axis=1, tiled=True),
    )
    return (full_parts, col_parts[3])


def fetch_backward(w_qkv, w_out, w_router, w_in, w_down):
    col_parts = (
        lax.all_gather(w_qkv, "expert", axis=1, tiled=True),
        lax.all_gather(w_out, "expert", axis=1, tiled=True),
        lax.all_gather(w_router, "expert", axis=1, tiled=True),
    )
    return (
        lax.all_gather(col_parts[0], "dp", axis=0, tiled=True),
        lax.all_gather(col_parts[1], "dp", axis=0, tiled=True),
        lax.all_gather(col_parts[2], "dp", axis=0, tiled=True),
        lax.all_gather(w_in, "dp", axis=2, tiled=True),
        lax.all_gather(w_down, "dp", axis=1, tiled=True),
    )


def shards(tokens, w_qkv, w_out, w_router, norm_params, w_in, w_down, routes, threshold, cotangent):
    tok_count = tokens.shape[0]
    images = tok_count // SEQ
    experts = lax.axis_size("expert")
    top_count = routes.shape[1]
    capacity = 15 * top_count * tok_count // (8 * experts)
    full_parts, norm_gains = fetch_forward(w_qkv, w_out, w_router, norm_params, w_in, w_down)
    full_qkv, full_out, full_router, full_in, full_down = full_parts
    gain_rows = norm_gains.astype(jnp.float32)
    source = tokens.astype(jnp.float32)
    first_norm, normed_one, inverse_one = layer_norm(source, gain_rows[0], gain_rows[1])
    first_low = first_norm.astype(jnp.bfloat16)
    qkv_rows = jnp.dot(first_low, full_qkv, preferred_element_type=jnp.float32).astype(jnp.bfloat16)
    qkv_split = qkv_rows.reshape(images, SEQ, 3, HEADS, HEAD)
    queries, key_part, values = (qkv_split[:, :, 0], qkv_split[:, :, 1], qkv_split[:, :, 2])
    scores = scores_of(queries, key_part)
    head_peaks = jnp.max(scores, axis=(0, 2, 3))
    row_peak = jnp.max(scores, axis=-1, keepdims=True)
    log_total = row_peak + jnp.log(jnp.sum(jnp.exp(scores - row_peak), axis=-1, keepdims=True))
    probs_low = jnp.exp(scores - log_total).astype(jnp.bfloat16)
    attn_mixed = jnp.einsum(
        "bhqk,bkhd->bqhd", probs_low, values, preferred_element_type=jnp.float32
    )
    attn_mixed = attn_mixed.reshape(tok_count, D).astype(jnp.bfloat16)
    resid = source + jnp.dot(attn_mixed, full_out, preferred_element_type=jnp.float32)
    peak_logit = lax.pmax(head_peaks, ("dp", "expert"))
    second_norm, normed_two, inverse_two = layer_norm(resid, gain_rows[2], gain_rows[3])
    second_low = second_norm.astype(jnp.bfloat16)
    logits = jnp.dot(second_low, full_router, preferred_element_type=jnp.float32)
    router_probs = jax.nn.softmax(logits, axis=-1)
    expert_ids = jnp.arange(experts, dtype=jnp.int32)
    chosen = (routes[:, :, None] == expert_ids[None, None, :]).astype(jnp.float32)
    gate_weights = jnp.sum(chosen * router_probs[:, None, :], axis=-1)
    flat_routes = routes.reshape(-1)
    onehot = (flat_routes[:, None] == expert_ids[None, :]).astype(jnp.int32)
    count = flat_routes.shape[0]
    earlier = jnp.tril(jnp.ones((count, count), jnp.bfloat16), -1)
    before = jnp.dot(
        earlier, onehot.astype(jnp.bfloat16), preferred_element_type=jnp.float32
    ).astype(jnp.int32)
    target_slot = flat_routes * capacity + jnp.sum(before * onehot, axis=1)
    routed = jnp.repeat(second_low, top_count, axis=0)
    outgoing = jnp.zeros((experts * capacity, D), jnp.bfloat16).at[target_slot].set(routed)
    arrived = lax.all_to_all(
        outgoing.reshape(experts, capacity, D), "expert", split_axis=0, concat_axis=0, tiled=True
    )
    arrived = arrived.reshape(experts * capacity, D)
    hidden = jnp.dot(arrived, full_in[0], preferred_element_type=jnp.float32)
    active, gelu_back = jax.vjp(exact_gelu, hidden)
    active_low = active.astype(jnp.bfloat16)
    expert_out = jnp.dot(active_low, full_down[0], preferred_element_type=jnp.float32).astype(
        jnp.bfloat16
    )
    returned = lax.all_to_all(
        expert_out.reshape(experts, capacity, D), "expert", split_axis=0, concat_axis=0, tiled=True
    )
    picked = (
        returned.reshape(experts * capacity, D)[target_slot]
        .astype(jnp.float32)
        .reshape(tok_count, top_count, D)
    )
    output = resid + jnp.sum(picked * gate_weights[:, :, None], axis=1)
    upstream = cotangent.astype(jnp.float32)
    anchor, upstream = lax.optimization_barrier(((w_qkv, w_out, w_router, w_in, w_down), upstream))
    back_qkv, back_out, back_router, back_in, back_down = fetch_backward(
        anchor[0], anchor[1], anchor[2], anchor[3], anchor[4]
    )
    grad_picked = (
        (upstream[:, None, :] * gate_weights[:, :, None])
        .astype(jnp.bfloat16)
        .reshape(tok_count * top_count, D)
    )
    grad_gates = jnp.sum(upstream[:, None, :] * picked, axis=-1)
    grad_probs = jnp.sum(grad_gates[:, :, None] * chosen, axis=1)
    grad_logits = router_probs * (
        grad_probs - jnp.sum(grad_probs * router_probs, axis=-1, keepdims=True)
    )
    back_slots = jnp.zeros((experts * capacity, D), jnp.bfloat16).at[target_slot].set(grad_picked)
    grad_expert = lax.all_to_all(
        back_slots.reshape(experts, capacity, D), "expert", split_axis=0, concat_axis=0, tiled=True
    )
    grad_expert = grad_expert.reshape(experts * capacity, D)
    grad_down = contract_rows(active_low, grad_expert)
    grad_active = contract_cols(grad_expert, back_down[0])
    grad_hidden = gelu_back(grad_active)[0].astype(jnp.bfloat16)
    grad_in = contract_rows(arrived, grad_hidden)
    grad_rows = contract_cols(grad_hidden, back_in[0]).astype(jnp.bfloat16)
    grad_back = lax.all_to_all(
        grad_rows.reshape(experts, capacity, D), "expert", split_axis=0, concat_axis=0, tiled=True
    )
    grad_routed = grad_back.reshape(experts * capacity, D)[target_slot].astype(jnp.float32)
    router_float = back_router.astype(jnp.float32)
    grad_second = jnp.sum(grad_routed.reshape(tok_count, top_count, D), axis=1) + lax.dot_general(
        grad_logits, router_float, (((1,), (1,)), ((), ())), precision=lax.Precision.HIGHEST
    )
    grad_router = lax.dot_general(
        second_low.astype(jnp.float32),
        grad_logits,
        (((0,), (0,)), ((), ())),
        precision=lax.Precision.HIGHEST,
    )
    grad_resid_two, gain_two_grad, shift_two_grad = plain_norm_back(
        grad_second, normed_two, inverse_two, gain_rows[2]
    )
    grad_resid = upstream + grad_resid_two
    grad_resid_low = grad_resid.astype(jnp.bfloat16)
    grad_out = contract_rows(attn_mixed, grad_resid_low)
    grad_mixed = (
        contract_cols(grad_resid_low, back_out)
        .astype(jnp.bfloat16)
        .reshape(images, SEQ, HEADS, HEAD)
    )
    again_scores = scores_of(queries, key_part)
    probs_full = jnp.exp(again_scores - log_total)
    grad_attn = jnp.einsum(
        "bqhd,bkhd->bhqk", grad_mixed, values, preferred_element_type=jnp.float32
    )
    grad_scores = (
        probs_full * (grad_attn - jnp.sum(grad_attn * probs_full, axis=-1, keepdims=True))
    ).astype(jnp.bfloat16)
    grad_queries = jnp.einsum(
        "bhqk,bkhd->bqhd", grad_scores, key_part, preferred_element_type=jnp.float32
    ) * HEAD ** (-0.5)
    grad_keys = jnp.einsum(
        "bhqk,bqhd->bkhd", grad_scores, queries, preferred_element_type=jnp.float32
    ) * HEAD ** (-0.5)
    grad_values = jnp.einsum(
        "bhqk,bqhd->bkhd", probs_low, grad_mixed, preferred_element_type=jnp.float32
    )
    grad_qkv_rows = (
        jnp.stack([grad_queries, grad_keys, grad_values], axis=2)
        .reshape(tok_count, 3 * D)
        .astype(jnp.bfloat16)
    )
    grad_qkv = contract_rows(first_low, grad_qkv_rows)
    grad_first = contract_cols(grad_qkv_rows, back_qkv)
    grad_source, gain_one_grad, shift_one_grad = plain_norm_back(
        grad_first, normed_one, inverse_one, gain_rows[0]
    )
    grad_tokens = (grad_resid + grad_source).astype(jnp.bfloat16)
    norm_grads = jnp.stack([gain_one_grad, shift_one_grad, gain_two_grad, shift_two_grad])
    col_sums = (
        lax.psum_scatter(
            grad_qkv.astype(jnp.bfloat16), "expert", scatter_dimension=1, tiled=True
        ).astype(jnp.float32),
        lax.psum_scatter(
            grad_out.astype(jnp.bfloat16), "expert", scatter_dimension=1, tiled=True
        ).astype(jnp.float32),
        lax.psum_scatter(
            grad_router.astype(jnp.bfloat16), "expert", scatter_dimension=1, tiled=True
        ).astype(jnp.float32),
        lax.psum_scatter(
            norm_grads.astype(jnp.bfloat16), "expert", scatter_dimension=1, tiled=True
        ).astype(jnp.float32),
    )
    row_sums = (
        lax.psum_scatter(
            col_sums[0].astype(jnp.bfloat16), "dp", scatter_dimension=0, tiled=True
        ).astype(jnp.float32),
        lax.psum_scatter(
            col_sums[1].astype(jnp.bfloat16), "dp", scatter_dimension=0, tiled=True
        ).astype(jnp.float32),
        lax.psum_scatter(
            col_sums[2].astype(jnp.bfloat16), "dp", scatter_dimension=0, tiled=True
        ).astype(jnp.float32),
        lax.psum_scatter(
            grad_in[None].astype(jnp.bfloat16), "dp", scatter_dimension=2, tiled=True
        ).astype(jnp.float32),
        lax.psum_scatter(
            grad_down[None].astype(jnp.bfloat16), "dp", scatter_dimension=1, tiled=True
        ).astype(jnp.float32),
    )
    norm_total = lax.psum(col_sums[3], "dp")
    factors = jnp.sqrt(jnp.minimum(1.0, threshold[0].astype(jnp.float32) / peak_logit))
    col_width = w_qkv.shape[1]
    column = lax.axis_index("expert") * col_width + jnp.arange(col_width, dtype=jnp.int32)
    head_index = column % D // HEAD
    head_table = jnp.sum(
        jnp.where(
            head_index[:, None] == jnp.arange(HEADS, dtype=jnp.int32)[None, :],
            factors[None, :],
            0.0,
        ),
        axis=1,
    )
    column_scale = jnp.where(column < 2 * D, head_table, 1.0)
    clipped = (w_qkv.astype(jnp.float32) - LEARN * row_sums[0]) * column_scale[None, :]
    return (
        output.astype(jnp.bfloat16),
        grad_tokens,
        row_sums[0],
        row_sums[1],
        row_sums[2],
        norm_total,
        row_sums[3],
        row_sums[4],
        clipped,
        factors,
    )


def solution(mesh):
    in_specs = (
        P(("dp", "expert"), None),
        P("dp", "expert"),
        P("dp", "expert"),
        P("dp", "expert"),
        P(None, "expert"),
        P("expert", None, "dp"),
        P("expert", "dp", None),
        P(("dp", "expert"), None),
        P(),
        P(("dp", "expert"), None),
    )
    out_specs = (
        P(("dp", "expert"), None),
        P(("dp", "expert"), None),
        P("dp", "expert"),
        P("dp", "expert"),
        P("dp", "expert"),
        P(None, "expert"),
        P("expert", None, "dp"),
        P("expert", "dp", None),
        P("dp", "expert"),
        P(),
    )
    fits = mesh.shape["dp"] == 4 and mesh.shape["expert"] == 8
    return jax.shard_map(fused if fits else shards, mesh=mesh, in_specs=in_specs, out_specs=out_specs, check_vma=False)
```
